32 devices in a mesh: ctx: 16 (over z, x, core), tp: 2 (over y).
Axes of the slice: x: 2, y: 2, z: 4, core: 2. Of those that a mesh axis runs over, the one named last changes fastest.
Arguments:
- tokens: bfloat16 [2, 1024, 768], P(None, 'ctx'), may hold values from -6 to 6
- out_grad: bfloat16 [2, 1024, 768], P(None, 'ctx'), may hold values from -6 to 6
- block_order: int32 [2, 32], replicated, may hold values from 0 to 31, as said below
- qkv_weight: float32 [768, 3, 768], P('ctx', None, 'tp'), may hold values from -0.21875 to 0.21875
- proj_weight: float32 [768, 768], P('tp', 'ctx'), may hold values from -2.5 to 2.5
- up_weight: float32 [768, 3072], P('ctx', 'tp'), may hold values from -0.21875 to 0.21875
- down_weight: float32 [3072, 768], P('tp', 'ctx'), may hold values from -0.109375 to 0.109375
- qkv_bias: float32 [2, 768], P(None, 'tp'), may hold values from -4 to 4
- up_bias: float32 [3072], P('tp'), may hold values from -4 to 4
- layer_vectors: float32 [6, 768], P(None, 'ctx'), may hold values from -2 to 2, as said below
- qkv_first: float32 [768, 3, 768], P('ctx', None, 'tp'), may hold values from -4 to 4
- qkv_second: float32 [768, 3, 768], P('ctx', None, 'tp'), may hold values from 9.216 to 73.728
- proj_first: float32 [768, 768], P('tp', 'ctx'), may hold values from -3.5 to 3.5
- proj_second: float32 [768, 768], P('tp', 'ctx'), may hold values from 0.256 to 2.048
- up_first: float32 [768, 3072], P('ctx', 'tp'), may hold values from -16 to 16
- up_second: float32 [768, 3072], P('ctx', 'tp'), may hold values from 25.6 to 204.8
- down_first: float32 [3072, 768], P('tp', 'ctx'), may hold values from -16 to 16
- down_second: float32 [3072, 768], P('tp', 'ctx'), may hold values from 25.6 to 204.8
- qbias_first: float32 [2, 768], P(None, 'tp'), may hold values from -4 to 4
- qbias_second: float32 [2, 768], P(None, 'tp'), may hold values from 9.216 to 73.728
- ubias_first: float32 [3072], P('tp'), may hold values from -16 to 16
- ubias_second: float32 [3072], P('tp'), may hold values from 25.6 to 204.8
- vector_first: float32 [6, 768], P(None, 'ctx'), may hold values from -32 to 32
- vector_second: float32 [6, 768], P(None, 'ctx'), may hold values from 102.4 to 819.2
Outputs:
- block_output: bfloat16 [2, 1024, 768], P(None, 'ctx')
- input_grad: float32 [2, 1024, 768], P(None, 'ctx')
- qkv_next: float32 [768, 3, 768], P('ctx', None, 'tp')
- qkvfirst_next: float32 [768, 3, 768], P('ctx', None, 'tp')
- qkvsecond_next: float32 [768, 3, 768], P('ctx', None, 'tp')
- proj_next: float32 [768, 768], P('tp', 'ctx')
- projfirst_next: float32 [768, 768], P('tp', 'ctx')
- projsecond_next: float32 [768, 768], P('tp', 'ctx')
- up_next: float32 [768, 3072], P('ctx', 'tp')
- upfirst_next: float32 [768, 3072], P('ctx', 'tp')
- upsecond_next: float32 [768, 3072], P('ctx', 'tp')
- down_next: float32 [3072, 768], P('tp', 'ctx')
- downfirst_next: float32 [3072, 768], P('tp', 'ctx')
- downsecond_next: float32 [3072, 768], P('tp', 'ctx')
- qbias_next: float32 [2, 768], P(None, 'tp')
- qbiasfirst_next: float32 [2, 768], P(None, 'tp')
- qbiassecond_next: float32 [2, 768], P(None, 'tp')
- ubias_next: float32 [3072], P('tp')
- ubiasfirst_next: float32 [3072], P('tp')
- ubiassecond_next: float32 [3072], P('tp')
- vector_next: float32 [6, 768], P(None, 'ctx')
- vectorfirst_next: float32 [6, 768], P(None, 'ctx')
- vectorsecond_next: float32 [6, 768], P(None, 'ctx')
The draws below stay inside these ranges and needn't reach their ends.
Inputs may be any that keep to these rules, and one draw needn't show every extreme that they name: `block_order`: each row is a permutation of the block numbers; entries 2 d and 2 d + 1 of a row add up to 31. `layer_vectors`: rows 0 and 2 lie within 0.7 to 1.3.
All inputs are finite; a program needn't handle non-finite values.
Results may differ from the reference program's by a relative error of at most 0.02.
Values may be sent and summed in bfloat16 or wider, within the bound.
A program may use at most 192 MiB of HBM per device.

```python
import math
import jax
import jax.numpy as jnp
from jax import lax

D = 768
HEADS = 12
HD = 64
FF = 3072
SEQS = 2
BLK = 32
STEP = 10
NBLK = 32
LEN = 1024
TOKENS = 2048


def draw_block_order(key, part):
    key = jax.random.fold_in(key, 17)
    order_key, flip_key = jax.random.split(key)
    half = NBLK // 2

    def ranking(single):
        return jax.random.permutation(single, half)
    ranks = jax.vmap(ranking)(jax.random.split(order_key, SEQS)).astype(jnp.int32)
    flips = jax.random.randint(flip_key, (SEQS, half), 0, 2)
    first = jnp.where(flips == 1, NBLK - 1 - ranks, ranks)
    return jnp.stack([first, NBLK - 1 - first], axis=-1).reshape(SEQS, NBLK).astype(jnp.int32)


def draw_layer_vectors(key, part):
    key = jax.random.fold_in(key, 29)
    gain_key, shift_key, bias_key = jax.random.split(key, 3)
    gains = 1.0 + 0.3 * jax.random.uniform(gain_key, (2, D), jnp.float32, -1.0, 1.0)
    shifts = 0.2 * jnp.clip(jax.random.normal(shift_key, (2, D), jnp.float32), -4.0, 4.0)
    biases = 0.3 * jnp.clip(jax.random.normal(bias_key, (2, D), jnp.float32), -4.0, 4.0)
    return jnp.stack([gains[0], shifts[0], gains[1], shifts[1], biases[0], biases[1]]).astype(jnp.float32)


def block_scale(rng, dims, cuts, smallest, high):
    loudness, own = 1.0, jax.random.fold_in(rng, 6)
    for axis_at, shards_of in cuts:
        steps = jnp.exp(jax.random.uniform(jax.random.fold_in(own, axis_at), (shards_of,), jnp.float32, smallest / len(cuts), high / len(cuts)))
        loudness = loudness * jnp.repeat(steps, dims[axis_at] // shards_of).reshape([-1 if axis == axis_at else 1 for axis in range(len(dims))])
    return loudness


def normal_values(stream_key, extent, width, bound, shards=(), held_as=jnp.bfloat16):
    array = jax.random.normal(stream_key, extent, jnp.float32) * width
    if len(shards) > 0:
        array = block_scale(stream_key, extent, shards, -0.22, 0.18) * array
    return jnp.clip(array, min=-bound, max=bound).astype(held_as)


def setup_inputs(seed: int = 0) -> dict:
    key_list = jax.random.split(jax.random.key(seed), 25)
    return {
        "tokens": normal_values(key_list[0], (SEQS, LEN, D), 1.0, 6.0, ((1, 16),)),
        "out_grad": normal_values(key_list[1], (SEQS, LEN, D), 1.0, 6.0, ((1, 16),)),
        "block_order": draw_block_order(jax.random.fold_in(key_list[24], 71), 0),
        "qkv_weight": normal_values(key_list[3], (D, 3, D), D ** -0.5, 0.21875, ((0, 16), (2, 2)), jnp.float32),
        "proj_weight": normal_values(key_list[4], (D, D), ((LEN / 32768) ** 0.5), 2.5, ((0, 2), (1, 16)), jnp.float32),
        "up_weight": normal_values(key_list[5], (D, FF), D ** -0.5, 0.21875, ((0, 16), (1, 2)), jnp.float32),
        "down_weight": normal_values(key_list[6], (FF, D), FF ** -0.5, 0.109375, ((0, 2), (1, 16)), jnp.float32),
        "qkv_bias": normal_values(key_list[7], (2, D), 0.3, 4.0, ((1, 2),), jnp.float32),
        "up_bias": normal_values(key_list[8], (FF,), 0.3, 4.0, ((0, 2),), jnp.float32),
        "layer_vectors": draw_layer_vectors(jax.random.fold_in(key_list[24], 71), 0),
        "qkv_first": normal_values(key_list[10], (D, 3, D), (0.033 * TOKENS ** 0.5), 4.0, ((0, 16), (2, 2)), jnp.float32),
        "qkv_second": jnp.clip(jnp.exp(math.log(73.728) - 2.0794415 * jax.random.uniform(key_list[11], (D, 3, D), jnp.float32) ** block_scale(key_list[11], (D, 3, D), ((0, 16), (2, 2)), -0.2, 0.2)), 9.216, 73.728),
        "proj_first": normal_values(key_list[12], (D, D), (0.0055 * TOKENS ** 0.5), 3.5, ((0, 2), (1, 16)), jnp.float32),
        "proj_second": jnp.clip(jnp.exp(math.log(2.048) - 2.0794415 * jax.random.uniform(key_list[13], (D, D), jnp.float32) ** block_scale(key_list[13], (D, D), ((0, 2), (1, 16)), -0.2, 0.2)), 0.256, 2.048),
        "up_first": normal_values(key_list[14], (D, FF), (0.055 * TOKENS ** 0.5), 16.0, ((0, 16), (1, 2)), jnp.float32),
        "up_second": jnp.clip(jnp.exp(math.log(204.8) - 2.0794415 * jax.random.uniform(key_list[15], (D, FF), jnp.float32) ** block_scale(key_list[15], (D, FF), ((0, 16), (1, 2)), -0.2, 0.2)), 25.6, 204.8),
        "down_first": normal_values(key_list[16], (FF, D), (0.055 * TOKENS ** 0.5), 16.0, ((0, 2), (1, 16)), jnp.float32),
        "down_second": jnp.clip(jnp.exp(math.log(204.8) - 2.0794415 * jax.random.uniform(key_list[17], (FF, D), jnp.float32) ** block_scale(key_list[17], (FF, D), ((0, 2), (1, 16)), -0.2, 0.2)), 25.6, 204.8),
        "qbias_first": normal_values(key_list[18], (2, D), (0.033 * TOKENS ** 0.5), 4.0, ((1, 2),), jnp.float32),
        "qbias_second": jnp.clip(jnp.exp(math.log(73.728) - 2.0794415 * jax.random.uniform(key_list[19], (2, D), jnp.float32) ** block_scale(key_list[19], (2, D), ((1, 2),), -0.2, 0.2)), 9.216, 73.728),
        "ubias_first": normal_values(key_list[20], (FF,), (0.055 * TOKENS ** 0.5), 16.0, ((0, 2),), jnp.float32),
        "ubias_second": jnp.clip(jnp.exp(math.log(204.8) - 2.0794415 * jax.random.uniform(key_list[21], (FF,), jnp.float32) ** block_scale(key_list[21], (FF,), ((0, 2),), -0.2, 0.2)), 25.6, 204.8),
        "vector_first": normal_values(key_list[22], (6, D), (0.11 * TOKENS ** 0.5), 32.0, ((1, 16),), jnp.float32),
        "vector_second": jnp.clip(jnp.exp(math.log(819.2) - 2.0794415 * jax.random.uniform(key_list[23], (6, D), jnp.float32) ** block_scale(key_list[23], (6, D), ((1, 16),), -0.2, 0.2)), 102.4, 819.2),
    }


@jax.custom_vjp
def low(v):
    return lax.optimization_barrier(v.astype(jnp.bfloat16)).astype(jnp.float32)

@jax.custom_vjp
def low_back(v):
    return v

def low_keep(v):
    return (low(v), None)

def low_pass(kept, grad):
    return (grad,)

def back_keep(v):
    return (v, None)

def back_low(kept, grad):
    return (low(grad),)
low.defvjp(low_keep, low_pass)
low_back.defvjp(back_keep, back_low)
exact_precision = lax.Precision.HIGHEST
BETA_ONE = 0.9
BETA_TWO = 0.95
EPSILON = 1e-08

def layer_norm(values, gain, shift):
    center = values - lax.optimization_barrier(jnp.mean(values, axis=-1, keepdims=True))
    spread = lax.optimization_barrier(jnp.mean(center * center, axis=-1, keepdims=True))
    return center * lax.rsqrt(spread + 1e-05) * gain + shift

def gelu_tanh(values):
    return 0.5 * values * (1.0 + jnp.tanh(0.7978845608028654 * (values + 0.044715 * values * values * values)))

def attention(queries, keys, values, positions):
    seqs, length = positions.shape
    rows = min(256, length)
    count = length // rows
    query_blocks = jnp.moveaxis(queries.reshape(seqs, count, rows, HEADS, HD), 1, 0)
    place_blocks = jnp.moveaxis(positions.reshape(seqs, count, rows), 1, 0)

    def one_block(pair):
        query_rows, query_place = pair
        scores = jnp.einsum('sqhd,skhd->shqk', query_rows, keys, precision=exact_precision) * 0.125
        allowed = query_place[:, None, :, None] >= positions[:, None, None, :]
        scores = low_back(jnp.where(allowed, scores, -1000000000.0))
        shares = low(jax.nn.softmax(scores, axis=-1))
        return jnp.einsum('shqk,skhd->sqhd', shares, values, precision=exact_precision)
    mixed = lax.map(jax.checkpoint(one_block), (query_blocks, place_blocks))
    return jnp.moveaxis(mixed, 0, 1).reshape(seqs, length, HEADS * HD)

def adamw(weight, grad, first, second, rate, decay):
    first_new = BETA_ONE * first + (1.0 - BETA_ONE) * grad
    second_new = BETA_TWO * second + (1.0 - BETA_TWO) * grad * grad
    first_hat = first_new / (1.0 - BETA_ONE ** STEP)
    second_hat = second_new / (1.0 - BETA_TWO ** STEP)
    weight_new = weight - rate * (first_hat / (jnp.sqrt(second_hat) + EPSILON) + decay * weight)
    return (weight_new, first_new, second_new)

def reference(tokens, out_grad, block_order, qkv_weight, proj_weight, up_weight, down_weight, qkv_bias, up_bias, layer_vectors, qkv_first, qkv_second, proj_first, proj_second, up_first, up_second, down_first, down_second, qbias_first, qbias_second, ubias_first, ubias_second, vector_first, vector_second):
    slots = jnp.arange(LEN, dtype=jnp.int32) // BLK
    offsets = jnp.arange(LEN, dtype=jnp.int32) % BLK
    positions = (jnp.take(block_order, slots, axis=1) * BLK + offsets[None, :]).astype(jnp.int32)
    seqs = tokens.shape[0]

    def forward(inputs, query_key_value_matrix, projection_matrix, up_matrix, down_matrix, qkv_b, up_offset_bias, layer_vector_rows):
        first_normalized = low(layer_norm(inputs, layer_vector_rows[0], layer_vector_rows[1]))
        projection_output = jnp.einsum('jar,rtz->jatz', first_normalized, low(query_key_value_matrix), precision=exact_precision)
        queries = low(low_back(projection_output[:, :, 0] + qkv_b[0]))
        keys = low(low_back(projection_output[:, :, 1]))
        values = low(low_back(projection_output[:, :, 2] + qkv_b[1]))
        context_value = attention(queries.reshape(seqs, LEN, HEADS, HD), keys.reshape(seqs, LEN, HEADS, HD), values.reshape(seqs, LEN, HEADS, HD), positions)
        context_value = low(low_back(context_value))
        attention_result = low_back(jnp.einsum('vnx,xm->vnm', context_value, low(projection_matrix), precision=exact_precision) + layer_vector_rows[4])
        middle = inputs + attention_result
        second_normalized = low(layer_norm(middle, layer_vector_rows[2], layer_vector_rows[3]))
        hidden_preactivation = low_back(jnp.einsum('rvk,ko->rvo', second_normalized, low(up_matrix), precision=exact_precision) + up_offset_bias)
        hidden_activation = low(gelu_tanh(hidden_preactivation))
        perceptron_output = low_back(jnp.einsum('vnx,xm->vnm', hidden_activation, low(down_matrix), precision=exact_precision) + layer_vector_rows[5])
        return middle + perceptron_output
    inputs = tokens.astype(jnp.float32)
    output, pullback = jax.vjp(forward, inputs, qkv_weight, proj_weight, up_weight, down_weight, qkv_bias, up_bias, layer_vectors)
    grads = pullback(out_grad.astype(jnp.float32))
    qkv_new = adamw(qkv_weight, grads[1], qkv_first, qkv_second, 0.1, 0.1)
    proj_new = adamw(proj_weight, grads[2], proj_first, proj_second, 1.0, 0.1)
    up_new = adamw(up_weight, grads[3], up_first, up_second, 0.1, 0.1)
    down_new = adamw(down_weight, grads[4], down_first, down_second, 0.05, 0.1)
    qbias_new = adamw(qkv_bias, grads[5], qbias_first, qbias_second, 1.0, 0.0)
    ubias_new = adamw(up_bias, grads[6], ubias_first, ubias_second, 1.0, 0.0)
    vector_new = adamw(layer_vectors, grads[7], vector_first, vector_second, 1.0, 0.0)
    return (output.astype(jnp.bfloat16), grads[0], qkv_new[0], qkv_new[1], qkv_new[2], proj_new[0], proj_new[1], proj_new[2], up_new[0], up_new[1], up_new[2], down_new[0], down_new[1], down_new[2], qbias_new[0], qbias_new[1], qbias_new[2], ubias_new[0], ubias_new[1], ubias_new[2], vector_new[0], vector_new[1], vector_new[2])
```

```python
from functools import partial
import math

import jax
import jax.numpy as jnp
from jax import lax
from jax.experimental import pallas as pl
from jax.experimental.pallas import tpu as pltpu
from jax.sharding import PartitionSpec as P

HD = 64
STEP = 10
WIDTH = 768
MESH = pl.DeviceIdType.MESH
VMEM_LIMIT = 48 * 1024 * 1024


BETA_ONE = 0.9
BETA_TWO = 0.95
EPSILON = 1e-08


def layer_norm(values, gain, shift):
    center = values - jnp.mean(values, axis=-1, keepdims=True)
    spread = jnp.mean(center * center, axis=-1, keepdims=True)
    return center * lax.rsqrt(spread + 1e-05) * gain + shift


def gelu_tanh(values):
    return (
        0.5
        * values
        * (1.0 + jnp.tanh(0.7978845608028654 * (values + 0.044715 * values * values * values)))
    )


def adamw(weight, grad, first, second, rate, decay):
    first_new = BETA_ONE * first + (1.0 - BETA_ONE) * grad
    second_new = BETA_TWO * second + (1.0 - BETA_TWO) * grad * grad
    first_hat = first_new / (1.0 - BETA_ONE**STEP)
    second_hat = second_new / (1.0 - BETA_TWO**STEP)
    weight_new = weight - rate * (first_hat / (jnp.sqrt(second_hat) + EPSILON) + decay * weight)
    return (weight_new, first_new, second_new)


def block_positions(order, start, count, blk):
    blocks = lax.dynamic_slice_in_dim(order, start // blk, count // blk, 1)
    offsets = jnp.arange(blk, dtype=jnp.int32)
    return (blocks[:, :, None] * blk + offsets[None, None, :]).reshape(order.shape[0], count)


def row_blocks(array, size):
    shape = array.shape
    return jnp.moveaxis(array.reshape((shape[0], shape[1] // size, size) + shape[2:]), 1, 0)


def forward_fold(carry, piece, start, queries, query_pos, order, blk):
    key_rows, value_rows = piece
    seqs, count, width = key_rows.shape
    heads = width // HD
    size = math.gcd(count, 512)
    key_pos = block_positions(order, start, count, blk)

    def step(state, block):
        key_block, value_block, place_block = block
        running_max, running_sum, context_sum = state
        key_heads = key_block.reshape(seqs, size, heads, HD)
        value_heads = value_block.reshape(seqs, size, heads, HD)
        scores = (
            jnp.einsum("sqhd,skhd->shqk", queries, key_heads, preferred_element_type=jnp.float32)
            * 0.125
        )
        allowed = query_pos[:, None, :, None] >= place_block[:, None, None, :]
        scores = jnp.where(allowed, scores, -1000000000.0)
        top_now = jnp.maximum(running_max, jnp.max(scores, axis=-1))
        rescale = jnp.exp(running_max - top_now)
        shares = jnp.exp(scores - top_now[..., None])
        running_sum = running_sum * rescale + jnp.sum(shares, axis=-1)
        context_sum = context_sum * rescale[..., None] + jnp.einsum(
            "shqk,skhd->shqd",
            shares.astype(jnp.bfloat16),
            value_heads,
            preferred_element_type=jnp.float32,
        )
        return ((top_now, running_sum, context_sum), None)

    carry, _ = lax.scan(
        step,
        carry,
        (row_blocks(key_rows, size), row_blocks(value_rows, size), row_blocks(key_pos, size)),
    )
    return carry


def keeping_fold(carry, piece, start, forward_step):
    state, key_store, value_store = carry
    key_rows, value_rows = piece
    key_store = key_rows
    value_store = value_rows
    state = forward_step(state, piece, start)
    return (state, key_store, value_store)


def query_fold(carry, piece, start, queries, grad_heads, log_total, delta, query_pos, order, blk):
    key_rows, value_rows = piece
    seqs, count, width = key_rows.shape
    heads = width // HD
    size = math.gcd(count, 512)
    key_pos = block_positions(order, start, count, blk)

    def step(grad_sum, block):
        key_block, value_block, place_block = block
        key_heads = key_block.reshape(seqs, size, heads, HD)
        value_heads = value_block.reshape(seqs, size, heads, HD)
        scores = (
            jnp.einsum("sqhd,skhd->shqk", queries, key_heads, preferred_element_type=jnp.float32)
            * 0.125
        )
        allowed = query_pos[:, None, :, None] >= place_block[:, None, None, :]
        scores = jnp.where(allowed, scores, -1000000000.0)
        shares = jnp.exp(scores - log_total[..., None])
        grad_share = jnp.einsum(
            "sqhd,skhd->shqk", grad_heads, value_heads, preferred_element_type=jnp.float32
        )
        grad_score = shares * (grad_share - delta[..., None])
        grad_sum = (
            grad_sum
            + jnp.einsum(
                "shqk,skhd->shqd",
                grad_score.astype(jnp.bfloat16),
                key_heads,
                preferred_element_type=jnp.float32,
            )
            * 0.125
        )
        return (grad_sum, None)

    carry, _ = lax.scan(
        step,
        carry,
        (row_blocks(key_rows, size), row_blocks(value_rows, size), row_blocks(key_pos, size)),
    )
    return carry


def key_fold(carry, piece, start, key_heads, value_heads, key_pos, order, blk):
    query_rows, grad_rows, log_rows, delta_rows = piece
    seqs, count, width = query_rows.shape
    heads = width // HD
    size = math.gcd(count, 512)
    query_pos = block_positions(order, start, count, blk)

    def step(state, block):
        grad_keys, grad_values = state
        query_block, grad_block, log_block, delta_block, place_block = block
        query_heads = query_block.reshape(seqs, size, heads, HD)
        grad_heads = grad_block.reshape(seqs, size, heads, HD)
        log_heads = jnp.transpose(log_block, (0, 2, 1))
        delta_heads = jnp.transpose(delta_block, (0, 2, 1))
        scores = (
            jnp.einsum(
                "sihd,sjhd->shij", query_heads, key_heads, preferred_element_type=jnp.float32
            )
            * 0.125
        )
        allowed = place_block[:, None, :, None] >= key_pos[:, None, None, :]
        scores = jnp.where(allowed, scores, -1000000000.0)
        shares = jnp.exp(scores - log_heads[..., None])
        grad_values = grad_values + jnp.einsum(
            "shij,sihd->shjd",
            shares.astype(jnp.bfloat16),
            grad_heads,
            preferred_element_type=jnp.float32,
        )
        grad_share = jnp.einsum(
            "sihd,sjhd->shij", grad_heads, value_heads, preferred_element_type=jnp.float32
        )
        grad_score = shares * (grad_share - delta_heads[..., None])
        grad_keys = (
            grad_keys
            + jnp.einsum(
                "shij,sihd->shjd",
                grad_score.astype(jnp.bfloat16),
                query_heads,
                preferred_element_type=jnp.float32,
            )
            * 0.125
        )
        return ((grad_keys, grad_values), None)

    carry, _ = lax.scan(
        step,
        carry,
        (
            row_blocks(query_rows, size),
            row_blocks(grad_rows, size),
            row_blocks(log_rows, size),
            row_blocks(delta_rows, size),
            row_blocks(query_pos, size),
        ),
    )
    return carry


def local(
    tokens,
    out_grad,
    block_order,
    qkv_weight,
    proj_weight,
    up_weight,
    down_weight,
    qkv_bias,
    up_bias,
    layer_vectors,
    qkv_first,
    qkv_second,
    proj_first,
    proj_second,
    up_first,
    up_second,
    down_first,
    down_second,
    qbias_first,
    qbias_second,
    ubias_first,
    ubias_second,
    vector_first,
    vector_second,
):
    device = lax.axis_index("ctx")
    groups = lax.axis_size("ctx")
    seqs, rows, width = tokens.shape
    blk = rows // 2
    query_pos = block_positions(block_order, device * rows, rows, blk)
    qkv_full, up_full, proj_full, down_full = (
        lax.all_gather(qkv_weight.astype(jnp.bfloat16), "ctx", axis=0, tiled=True),
        lax.all_gather(up_weight.astype(jnp.bfloat16), "ctx", axis=0, tiled=True),
        lax.all_gather(proj_weight.astype(jnp.bfloat16), "ctx", axis=1, tiled=True),
        lax.all_gather(down_weight.astype(jnp.bfloat16), "ctx", axis=1, tiled=True),
    )
    layer_vector_rows = lax.all_gather(layer_vectors, "ctx", axis=1, tiled=True)
    inputs = tokens.astype(jnp.float32)
    first_normalized, norm_one_back = jax.vjp(
        layer_norm, inputs, layer_vector_rows[0], layer_vector_rows[1]
    )
    normed_low = first_normalized.astype(jnp.bfloat16)
    projection_output = jnp.einsum(
        "sqd,dcf->sqcf", normed_low, qkv_full, preferred_element_type=jnp.float32
    )
    queries = (projection_output[:, :, 0] + qkv_bias[0]).astype(jnp.bfloat16)
    keys = projection_output[:, :, 1].astype(jnp.bfloat16)
    values = (projection_output[:, :, 2] + qkv_bias[1]).astype(jnp.bfloat16)
    heads = queries.shape[-1] // HD
    query_heads = queries.reshape(seqs, rows, heads, HD)
    key_heads = keys.reshape(seqs, rows, heads, HD)
    value_heads = values.reshape(seqs, rows, heads, HD)
    start_state = (
        jnp.full((seqs, heads, rows), -1e30, jnp.float32),
        jnp.zeros((seqs, heads, rows), jnp.float32),
        jnp.zeros((seqs, heads, rows, HD), jnp.float32),
    )
    forward_step = partial(
        forward_fold, queries=query_heads, query_pos=query_pos, order=block_order, blk=blk
    )
    empty_store = jnp.zeros((seqs, rows * groups, keys.shape[-1]), jnp.bfloat16)
    folded, key_store, value_store = keeping_fold(
        (start_state, empty_store, empty_store),
        (
            lax.all_gather(keys, "ctx", axis=1, tiled=True),
            lax.all_gather(values, "ctx", axis=1, tiled=True),
        ),
        jnp.int32(0),
        forward_step=forward_step,
    )
    running_max, running_sum, context_sum = folded
    whole_pair = (key_store, value_store)
    log_total = running_max + jnp.log(running_sum)
    context_value = context_sum / running_sum[..., None]
    context_rows = jnp.transpose(context_value, (0, 2, 1, 3)).reshape(seqs, rows, heads * HD)
    context_low = context_rows.astype(jnp.bfloat16)
    attn_part = jnp.einsum(
        "sqf,fd->sqd", context_low, proj_full, preferred_element_type=jnp.float32
    )
    attention_result = lax.psum(attn_part, "tp") + layer_vector_rows[4]
    middle = inputs + attention_result
    second_normalized, norm_two_back = jax.vjp(
        layer_norm, middle, layer_vector_rows[2], layer_vector_rows[3]
    )
    normed_mid = second_normalized.astype(jnp.bfloat16)
    hidden_preactivation = (
        jnp.einsum("sqd,df->sqf", normed_mid, up_full, preferred_element_type=jnp.float32) + up_bias
    )
    hidden_activation, gelu_back = jax.vjp(gelu_tanh, hidden_preactivation)
    hidden_low = hidden_activation.astype(jnp.bfloat16)
    mlp_part = jnp.einsum("sqf,fd->sqd", hidden_low, down_full, preferred_element_type=jnp.float32)
    mlp_total = lax.psum(mlp_part, "tp") + layer_vector_rows[5]
    block_output = (middle + mlp_total).astype(jnp.bfloat16)
    grad_out = out_grad.astype(jnp.float32)
    grad_down = jnp.einsum("sqf,sqd->fd", hidden_low, out_grad, preferred_element_type=jnp.float32)
    grad_hidden = jnp.einsum("sqd,fd->sqf", out_grad, down_full, preferred_element_type=jnp.float32)
    grad_pre = gelu_back(grad_hidden)[0].astype(jnp.bfloat16)
    grad_up = jnp.einsum("sqd,sqf->df", normed_mid, grad_pre, preferred_element_type=jnp.float32)
    grad_upbias = jnp.sum(grad_pre.astype(jnp.float32), axis=(0, 1))
    mid_part = jnp.einsum("sqf,df->sqd", grad_pre, up_full, preferred_element_type=jnp.float32)
    grad_normed_two = lax.psum(mid_part, "tp")
    grad_mid_norm, grad_gain_two, grad_shift_two = norm_two_back(grad_normed_two)
    grad_middle = grad_out + grad_mid_norm
    grad_attn = grad_middle.astype(jnp.bfloat16)
    grad_proj = jnp.einsum(
        "sqf,sqd->fd", context_low, grad_attn, preferred_element_type=jnp.float32
    )
    grad_context = jnp.einsum(
        "sqd,fd->sqf", grad_attn, proj_full, preferred_element_type=jnp.float32
    ).astype(jnp.bfloat16)
    grad_heads = grad_context.reshape(seqs, rows, heads, HD)
    row_delta = jnp.sum(
        grad_heads.astype(jnp.float32) * context_rows.reshape(seqs, rows, heads, HD), axis=-1
    )
    delta_heads = jnp.transpose(row_delta, (0, 2, 1))
    log_rows = jnp.transpose(log_total, (0, 2, 1))
    zero_heads = jnp.zeros((seqs, heads, rows, HD), jnp.float32)
    query_step = partial(
        query_fold,
        queries=query_heads,
        grad_heads=grad_heads,
        log_total=log_total,
        delta=delta_heads,
        query_pos=query_pos,
        order=block_order,
        blk=blk,
    )
    grad_q_sum = query_step(zero_heads, whole_pair, 0)
    key_step = partial(
        key_fold,
        key_heads=key_heads,
        value_heads=value_heads,
        key_pos=query_pos,
        order=block_order,
        blk=blk,
    )
    grad_k_sum, grad_v_sum = key_step(
        (zero_heads, zero_heads),
        (
            lax.all_gather(queries.astype(jnp.float32), "ctx", axis=1, tiled=True).astype(
                jnp.bfloat16
            ),
            lax.all_gather(grad_context.astype(jnp.float32), "ctx", axis=1, tiled=True).astype(
                jnp.bfloat16
            ),
            lax.all_gather(log_rows, "ctx", axis=1, tiled=True),
            lax.all_gather(row_delta, "ctx", axis=1, tiled=True),
        ),
        jnp.int32(0),
    )

    def head_rows(array):
        return (
            jnp.transpose(array, (0, 2, 1, 3)).reshape(seqs, rows, heads * HD).astype(jnp.bfloat16)
        )

    grad_qkv_low = jnp.stack(
        [head_rows(grad_q_sum), head_rows(grad_k_sum), head_rows(grad_v_sum)], axis=2
    )
    grad_qkv = jnp.einsum(
        "sqd,sqcf->dcf", normed_low, grad_qkv_low, preferred_element_type=jnp.float32
    )
    grad_qbias = jnp.sum(grad_qkv_low[:, :, 0::2].astype(jnp.float32), axis=(0, 1))
    first_part = jnp.einsum(
        "sqcf,dcf->sqd", grad_qkv_low, qkv_full, preferred_element_type=jnp.float32
    )
    grad_normed_one = lax.psum(first_part, "tp")
    grad_in_norm, grad_gain_one, grad_shift_one = norm_one_back(grad_normed_one)
    input_grad = grad_middle + grad_in_norm
    grad_vectors = jnp.stack(
        [
            grad_gain_one,
            grad_shift_one,
            grad_gain_two,
            grad_shift_two,
            jnp.sum(grad_attn.astype(jnp.float32), axis=(0, 1)),
            jnp.sum(grad_out, axis=(0, 1)),
        ]
    )
    sum_qkv, sum_up, sum_proj, sum_down, sum_vectors = (
        lax.psum_scatter(grad_qkv, "ctx", scatter_dimension=0, tiled=True),
        lax.psum_scatter(grad_up, "ctx", scatter_dimension=0, tiled=True),
        lax.psum_scatter(grad_proj, "ctx", scatter_dimension=1, tiled=True),
        lax.psum_scatter(grad_down, "ctx", scatter_dimension=1, tiled=True),
        lax.psum_scatter(grad_vectors, "ctx", scatter_dimension=1, tiled=True),
    )
    sum_qbias, sum_upbias = lax.psum((grad_qbias, grad_upbias), "ctx")
    qkv_new = adamw(qkv_weight, sum_qkv, qkv_first, qkv_second, 0.1, 0.1)
    proj_new = adamw(proj_weight, sum_proj, proj_first, proj_second, 1.0, 0.1)
    up_new = adamw(up_weight, sum_up, up_first, up_second, 0.1, 0.1)
    down_new = adamw(down_weight, sum_down, down_first, down_second, 0.05, 0.1)
    qbias_new = adamw(qkv_bias, sum_qbias, qbias_first, qbias_second, 1.0, 0.0)
    ubias_new = adamw(up_bias, sum_upbias, ubias_first, ubias_second, 1.0, 0.0)
    vector_new = adamw(layer_vectors, sum_vectors, vector_first, vector_second, 1.0, 0.0)
    return (
        block_output,
        input_grad,
        qkv_new[0],
        qkv_new[1],
        qkv_new[2],
        proj_new[0],
        proj_new[1],
        proj_new[2],
        up_new[0],
        up_new[1],
        up_new[2],
        down_new[0],
        down_new[1],
        down_new[2],
        qbias_new[0],
        qbias_new[1],
        qbias_new[2],
        ubias_new[0],
        ubias_new[1],
        ubias_new[2],
        vector_new[0],
        vector_new[1],
        vector_new[2],
    )


def chip_at(place, chips):
    half = chips // 2
    back = place // half
    return (1 - back) * 2 * place + back * (2 * (chips - 1 - place) + 1)


class Ring:
    def __init__(self, chips):
        me = lax.axis_index("ctx")
        self.chips, self.me = chips, me
        self.core = me % 2
        chip = me // 2
        along, across = chip // 2, chip % 2
        self.place = along + across * (chips - 1 - 2 * along)
        self.right, self.left = self.slot(1), self.slot(-1)
        self.mate = chip * 2 + 1 - self.core

    def slot(self, ahead, other=False):
        place = (self.place + ahead + 2 * self.chips) % self.chips
        core = 1 - self.core if other else self.core
        return chip_at(place, self.chips) * 2 + core

    def greet(self):
        barrier = pltpu.get_barrier_semaphore()
        for device in (self.left, self.right, self.mate):
            pl.semaphore_signal(barrier, inc=1, device_id={"ctx": device}, device_id_type=MESH)
        pl.semaphore_wait(barrier, 3)


def remote(src, dst, send, recv, device):
    return pltpu.make_async_remote_copy(
        src_ref=src,
        dst_ref=dst,
        send_sem=send,
        recv_sem=recv,
        device_id={"ctx": device},
        device_id_type=MESH,
    )


class Gather:
    def __init__(self, ring, ins, outs, sems):
        self.ring, self.ins, self.outs = ring, ins, outs
        self.ring_send, self.ring_recv, self.mate_send, self.mate_recv, self.own = sems
        self.far_right = ring.chips // 2
        self.far_left = ring.chips - 1 - self.far_right
        self.sent = []

    def hop(self, at, src, slot, index, device):
        copy = remote(
            src, self.outs[at].at[slot], self.ring_send.at[at, index],
            self.ring_recv.at[at, index], device,
        )
        return copy

    def pass_on(self, at, src, slot, index):
        copy = remote(
            src, self.outs[at].at[slot], self.mate_send.at[at, index],
            self.mate_recv.at[at, index], self.ring.mate,
        )
        return copy

    def go(self, copy):
        copy.start()
        self.sent.append(copy)

    def start(self):
        ring = self.ring
        for at, block in enumerate(self.ins):
            self.go(self.hop(at, block, ring.me, 0, ring.right))
            self.go(self.hop(at, block, ring.me, self.far_right, ring.left))
            self.go(self.pass_on(at, block, ring.me, 0))
            pltpu.make_async_copy(block, self.outs[at].at[ring.me], self.own.at[at]).start()

    def step(self, step):
        ring = self.ring
        for at in range(len(self.ins)):
            for sign, far, base, device in (
                (-1, self.far_right, 0, ring.right),
                (1, self.far_left, self.far_right, ring.left),
            ):
                if step >= far:
                    continue
                slot = ring.slot(sign * (step + 1))
                block = self.outs[at].at[slot]
                self.hop(at, block, slot, base + step, device).wait_recv()
                if step + 1 < far:
                    self.go(self.hop(at, block, slot, base + step + 1, device))
                self.go(self.pass_on(at, block, slot, 1 + base + step))

    def finish(self):
        ring = self.ring
        for at in range(len(self.ins)):
            order = [0] + [-(s + 1) for s in range(self.far_right)]
            order += [s + 1 for s in range(self.far_left)]
            for index, ahead in enumerate(order):
                slot = ring.slot(ahead, other=True)
                self.pass_on(at, self.outs[at].at[slot], slot, index).wait_recv()
            pltpu.make_async_copy(
                self.ins[at], self.outs[at].at[ring.me], self.own.at[at]
            ).wait()
        for copy in self.sent:
            copy.wait_send()


def gather_sems(count, chips):
    return [pltpu.SemaphoreType.DMA((count, chips))] * 4 + [pltpu.SemaphoreType.DMA((count,))]


def gather_kernel(chips, count, *refs):
    ins, outs, sems = refs[:count], refs[count : 2 * count], refs[2 * count :]
    ring = Ring(chips)
    ring.greet()
    gather = Gather(ring, ins, outs, sems)
    gather.start()
    for step in range(gather.far_right):
        gather.step(step)
    gather.finish()


def ring_gather(arrays, groups, collective):
    count, chips = len(arrays), groups // 2
    return pl.pallas_call(
        partial(gather_kernel, chips, count),
        out_shape=[jax.ShapeDtypeStruct((groups,) + a.shape, a.dtype) for a in arrays],
        in_specs=[pl.BlockSpec(memory_space=pl.ANY)] * count,
        out_specs=[pl.BlockSpec(memory_space=pl.ANY)] * count,
        scratch_shapes=gather_sems(count, chips),
        compiler_params=pltpu.CompilerParams(collective_id=collective, has_side_effects=True),
    )(*arrays)


def scatter_kernel(chips, pieces, *refs):
    grads, small = refs[0:4], refs[4]
    outs, small_out = refs[5:9], refs[9]
    mates, lands = refs[10:14], refs[14 : 14 + len(pieces)]
    rest = refs[14 + len(pieces) :]
    mate_send, mate_recv, ring_send, ring_recv = rest[:4]
    ring = Ring(chips)
    ring.greet()
    order = []
    for far in range(1, chips // 2):
        order += [-far, far]
    order += [chips // 2, 0]
    sent = []

    def to_mate(index, at):
        ahead = order[index]
        return remote(
            grads[at].at[ring.slot(ahead, other=True)], mates[at].at[index],
            mate_send.at[at, index], mate_recv.at[at, index], ring.mate,
        )

    arrived = set()

    def own_part(ahead, at, columns):
        ahead = (ahead + chips // 2 - 1) % chips - (chips // 2 - 1)
        index = order.index(ahead)
        if (index, at) not in arrived:
            arrived.add((index, at))
            to_mate(index, at).wait_recv()
        mine = grads[at][ring.slot(ahead), :, columns].astype(jnp.float32)
        return mine + mates[at][index, :, columns].astype(jnp.float32)

    for index in range(chips):
        for at in range(4):
            copy = to_mate(index, at)
            copy.start()
            sent.append(copy)
    gather = Gather(ring, [small], [small_out], rest[4:])
    gather.start()

    def hop(which, step, src):
        device = ring.right if pieces[which][3] > 0 else ring.left
        return remote(
            src, lands[which].at[step], ring_send.at[which, step],
            ring_recv.at[which, step], device,
        )

    for step in range(chips):
        for which, (at, first, count, sign) in enumerate(pieces):
            columns = slice(first, first + count)
            part = own_part(-sign * (step + 1), at, columns)
            if step > 0:
                hop(which, step - 1, lands[which].at[step]).wait_recv()
                part = part + lands[which][step - 1].astype(jnp.float32)
            if step < chips - 1:
                hold = lands[which].at[chips - 1 + step]
                hold[...] = part.astype(jnp.bfloat16)
                copy = hop(which, step, hold)
                copy.start()
                sent.append(copy)
            else:
                outs[at][:, columns] = part
        if step < gather.far_right:
            gather.step(step)
    gather.finish()
    for copy in sent:
        copy.wait_send()


def ring_scatter(grads, small, groups, collective):
    chips = groups // 2
    blocks = [g.reshape(groups, g.shape[0] // groups, g.shape[1]) for g in grads]
    rows = blocks[0].shape[1]
    qkv, proj, up, down = [b.shape[2] for b in blocks]
    right_up = up * 3 // 4 // 128 * 128
    pieces = (
        (0, 0, qkv, 1),
        (3, 0, down, -1),
        (2, 0, right_up, 1),
        (1, 0, proj, -1),
        (2, right_up, up - right_up, -1),
    )
    vmem = pl.BlockSpec(memory_space=pltpu.VMEM)
    hbm = pl.BlockSpec(memory_space=pl.ANY)
    dma = pltpu.SemaphoreType.DMA
    return pl.pallas_call(
        partial(scatter_kernel, chips, pieces),
        out_shape=[jax.ShapeDtypeStruct(b.shape[1:], jnp.float32) for b in blocks]
        + [jax.ShapeDtypeStruct((groups,) + small.shape, small.dtype)],
        in_specs=[vmem] * 4 + [hbm],
        out_specs=[vmem] * 4 + [hbm],
        scratch_shapes=[pltpu.VMEM((chips, rows, b.shape[2]), jnp.bfloat16) for b in blocks]
        + [pltpu.VMEM((2 * chips - 2, rows, p[2]), jnp.bfloat16) for p in pieces]
        + [dma((4, chips)), dma((4, chips))]
        + [dma((len(pieces), chips)), dma((len(pieces), chips))]
        + gather_sems(1, chips),
        compiler_params=pltpu.CompilerParams(
            collective_id=collective, has_side_effects=True, vmem_limit_bytes=VMEM_LIMIT
        ),
    )(*blocks, small)


def pair_kernel(count, *refs):
    ins, outs = refs[:count], refs[count : 2 * count]
    holds, lands = refs[2 * count : 3 * count], refs[3 * count : 4 * count]
    send, recv = refs[4 * count :]
    other = 1 - lax.axis_index("tp")
    barrier = pltpu.get_barrier_semaphore()
    pl.semaphore_signal(barrier, inc=1, device_id={"tp": other}, device_id_type=MESH)
    for at in range(count):
        holds[at][...] = ins[at][...].astype(jnp.bfloat16)
    pl.semaphore_wait(barrier, 1)
    copies = []
    for at in range(count):
        copy = pltpu.make_async_remote_copy(
            src_ref=holds[at], dst_ref=lands[at], send_sem=send.at[at], recv_sem=recv.at[at],
            device_id={"tp": other}, device_id_type=MESH,
        )
        copy.start()
        copies.append(copy)
    for at in range(count):
        copies[at].wait()
        outs[at][...] = holds[at][...].astype(jnp.float32) + lands[at][...].astype(jnp.float32)


def pair_sum(arrays, collective):
    count = len(arrays)
    vmem = pl.BlockSpec(memory_space=pltpu.VMEM)
    return pl.pallas_call(
        partial(pair_kernel, count),
        out_shape=[jax.ShapeDtypeStruct(a.shape, jnp.float32) for a in arrays],
        in_specs=[vmem] * count,
        out_specs=[vmem] * count,
        scratch_shapes=[pltpu.VMEM(a.shape, jnp.bfloat16) for a in arrays] * 2
        + [pltpu.SemaphoreType.DMA((count,))] * 2,
        compiler_params=pltpu.CompilerParams(
            collective_id=collective, has_side_effects=True, vmem_limit_bytes=VMEM_LIMIT
        ),
    )(*arrays)


NT = (((1,), (1,)), ((), ()))
NN = (((1,), (0,)), ((), ()))


def mul(left, right, dims):
    return lax.dot_general(left, right, dims, preferred_element_type=jnp.float32)


def attend_kernel(heads, q_ref, kv_ref, own_ref, all_ref, context_ref, log_ref):
    seqs = own_ref.shape[0]
    rows = q_ref.shape[0] // seqs
    width = heads * HD
    lanes = lax.broadcasted_iota(jnp.int32, (rows, 128), 1)
    for seq in range(seqs):
        here = slice(seq * rows, (seq + 1) * rows)
        allowed = own_ref[seq] >= all_ref[seq]
        logs = jnp.zeros((rows, 128), jnp.float32)
        for head in range(heads):
            at = slice(head * HD, (head + 1) * HD)
            past = slice(width + head * HD, width + (head + 1) * HD)
            keys = kv_ref[:, here, at].reshape(-1, HD)
            values = kv_ref[:, here, past].reshape(-1, HD)
            scores = mul(q_ref[here, at], keys, NT) * 0.125
            scores = jnp.where(allowed, scores, -1000000000.0)
            top = jnp.max(scores, axis=-1, keepdims=True)
            shares = jnp.exp(scores - top)
            total = jnp.sum(shares, axis=-1, keepdims=True)
            mixed = mul(shares.astype(jnp.bfloat16), values, NN)
            context_ref[here, at] = mixed / total
            logs = jnp.where(lanes == head, top + jnp.log(total), logs)
        log_ref[here, :] = logs


def attend(queries, pairs, own_pos, all_pos, heads):
    vmem = pl.BlockSpec(memory_space=pltpu.VMEM)
    return pl.pallas_call(
        partial(attend_kernel, heads),
        out_shape=[
            jax.ShapeDtypeStruct(queries.shape, jnp.float32),
            jax.ShapeDtypeStruct((queries.shape[0], 128), jnp.float32),
        ],
        in_specs=[vmem] * 4,
        out_specs=[vmem] * 2,
        compiler_params=pltpu.CompilerParams(vmem_limit_bytes=VMEM_LIMIT),
    )(queries, pairs, own_pos, all_pos)


def attend_back_kernel(
    heads, qg_ref, stat_ref, kv_ref, qgs_ref, stats_ref, own_ref, all_ref, out_ref
):
    seqs = own_ref.shape[0]
    rows = qg_ref.shape[0] // seqs
    width = heads * HD
    me = lax.axis_index("ctx")
    for seq in range(seqs):
        here = slice(seq * rows, (seq + 1) * rows)
        allowed = own_ref[seq] >= all_ref[seq]
        allowed_back = own_ref[seq] <= all_ref[seq]
        turned = stats_ref[:, here, :].reshape(-1, 128).T
        for head in range(heads):
            at = slice(head * HD, (head + 1) * HD)
            past = slice(width + head * HD, width + (head + 1) * HD)
            keys = kv_ref[:, here, at].reshape(-1, HD)
            values = kv_ref[:, here, past].reshape(-1, HD)
            scores = jnp.where(allowed, mul(qg_ref[here, at], keys, NT) * 0.125, -1000000000.0)
            shares = jnp.exp(scores - stat_ref[here, head : head + 1])
            grad_share = mul(qg_ref[here, past], values, NT)
            delta = stat_ref[here, heads + head : heads + head + 1]
            grad_score = (shares * (grad_share - delta)).astype(jnp.bfloat16)
            out_ref[here, at] = (mul(grad_score, keys, NN) * 0.125).astype(jnp.bfloat16)
            queries = qgs_ref[:, here, at].reshape(-1, HD)
            grads = qgs_ref[:, here, past].reshape(-1, HD)
            key, value = kv_ref[me, here, at], kv_ref[me, here, past]
            scores = jnp.where(allowed_back, mul(key, queries, NT) * 0.125, -1000000000.0)
            shares = jnp.exp(scores - turned[head : head + 1])
            grad_value = mul(shares.astype(jnp.bfloat16), grads, NN)
            grad_share = mul(value, grads, NT)
            grad_score = shares * (grad_share - turned[heads + head : heads + head + 1])
            grad_key = mul(grad_score.astype(jnp.bfloat16), queries, NN) * 0.125
            out_ref[here, past] = grad_key.astype(jnp.bfloat16)
            last = slice(2 * width + head * HD, 2 * width + (head + 1) * HD)
            out_ref[here, last] = grad_value.astype(jnp.bfloat16)


def attend_back(own, stats, pairs, all_own, all_stats, own_pos, all_pos, heads):
    vmem = pl.BlockSpec(memory_space=pltpu.VMEM)
    return pl.pallas_call(
        partial(attend_back_kernel, heads),
        out_shape=jax.ShapeDtypeStruct((own.shape[0], 3 * heads * HD), jnp.bfloat16),
        in_specs=[vmem] * 7,
        out_specs=vmem,
        compiler_params=pltpu.CompilerParams(vmem_limit_bytes=VMEM_LIMIT),
    )(own, stats, pairs, all_own, all_stats, own_pos, all_pos)


def three_parts(array):
    high = lax.reduce_precision(array, 8, 7)
    rest = array - high
    middle = lax.reduce_precision(rest, 8, 7)
    return [part.astype(jnp.bfloat16) for part in (high, middle, rest - middle)]


def ring_local(
    tokens,
    out_grad,
    block_order,
    qkv_weight,
    proj_weight,
    up_weight,
    down_weight,
    qkv_bias,
    up_bias,
    layer_vectors,
    qkv_first,
    qkv_second,
    proj_first,
    proj_second,
    up_first,
    up_second,
    down_first,
    down_second,
    qbias_first,
    qbias_second,
    ubias_first,
    ubias_second,
    vector_first,
    vector_second,
):
    device = lax.axis_index("ctx")
    groups = lax.axis_size("ctx")
    seqs, rows, width = tokens.shape
    blk = rows // 2
    share = qkv_weight.shape[0]
    inner = qkv_weight.shape[2]
    heads = inner // HD
    many = seqs * rows
    own_pos = block_positions(block_order, device * rows, rows, blk)[:, :, None]
    all_pos = block_positions(block_order, 0, rows * groups, blk)[:, None, :]
    low = jnp.bfloat16
    vector_parts = jnp.concatenate(three_parts(layer_vectors.T), axis=1)
    packed = jnp.concatenate(
        [
            qkv_weight.astype(low).reshape(share, 3 * inner),
            jnp.pad(vector_parts, ((0, 0), (0, 128 - vector_parts.shape[1]))),
        ],
        axis=1,
    )
    packed_full, proj_full, up_full, down_full = ring_gather(
        [packed, proj_weight.astype(low).T, up_weight.astype(low), down_weight.astype(low).T],
        groups,
        1,
    )
    packed_full = packed_full.reshape(width, -1)
    qkv_full = packed_full[:, : 3 * inner]
    vectors = packed_full[:, 3 * inner : 3 * inner + 18].astype(jnp.float32).T
    vectors = (vectors[0:6] + vectors[6:12]) + vectors[12:18]
    proj_full = proj_full.reshape(width, -1)
    up_full = up_full.reshape(width, -1)
    down_full = down_full.reshape(width, -1)
    inputs = tokens.reshape(many, width).astype(jnp.float32)
    grad_low = out_grad.reshape(many, width)
    first_normalized, norm_one_back = jax.vjp(layer_norm, inputs, vectors[0], vectors[1])
    normed_low = first_normalized.astype(low)
    projected = mul(normed_low, qkv_full, NN)
    bias = jnp.concatenate([qkv_bias[0], jnp.zeros_like(qkv_bias[0]), qkv_bias[1]])
    projected = (projected + bias).astype(low)
    queries = projected[:, :inner]
    (pairs,) = ring_gather([projected[:, inner:]], groups, 2)
    context, logs = attend(queries, pairs, own_pos, all_pos, heads)
    context_low = context.astype(low)
    (attn,) = pair_sum([mul(context_low, proj_full, NT)], 3)
    middle = inputs + (attn + vectors[4])
    second_normalized, norm_two_back = jax.vjp(layer_norm, middle, vectors[2], vectors[3])
    normed_mid = second_normalized.astype(low)
    hidden_preactivation = mul(normed_mid, up_full, NN) + up_bias
    hidden_activation, gelu_back = jax.vjp(gelu_tanh, hidden_preactivation)
    hidden_low = hidden_activation.astype(low)
    grad_hidden = mul(grad_low, down_full, NN)
    grad_pre = gelu_back(grad_hidden)[0].astype(low)
    mlp, grad_normed_two = pair_sum(
        [mul(hidden_low, down_full, NT), mul(grad_pre, up_full, NT)], 4
    )
    block_output = (middle + (mlp + vectors[5])).astype(low)
    grad_out = grad_low.astype(jnp.float32)
    grad_mid_norm, grad_gain_two, grad_shift_two = norm_two_back(grad_normed_two)
    grad_middle = grad_out + grad_mid_norm
    grad_attn = grad_middle.astype(low)
    grad_context = mul(grad_attn, proj_full, NN).astype(low)
    lanes = jnp.arange(128)[None, :]
    choose = (lanes == heads + jnp.arange(inner)[:, None] // HD).astype(jnp.float32)
    delta = jnp.dot(
        grad_context.astype(jnp.float32) * context, choose, precision=lax.Precision.HIGHEST
    )
    stats = logs + delta
    own = jnp.concatenate([queries, grad_context], axis=1)
    all_own, all_stats = ring_gather([own, stats], groups, 5)
    grad_low_qkv = attend_back(own, stats, pairs, all_own, all_stats, own_pos, all_pos, heads)
    (grad_normed_one,) = pair_sum([mul(grad_low_qkv, qkv_full, NT)], 6)
    grad_in_norm, grad_gain_one, grad_shift_one = norm_one_back(grad_normed_one)
    input_grad = grad_middle + grad_in_norm

    def turned(left, right):
        return lax.dot_general(
            left, right, (((0,), (0,)), ((), ())), preferred_element_type=jnp.float32
        ).astype(low)

    grad_qbias = jnp.sum(grad_low_qkv.astype(jnp.float32), axis=0)
    small = jnp.concatenate(
        [
            grad_gain_one,
            grad_shift_one,
            grad_gain_two,
            grad_shift_two,
            jnp.sum(grad_attn.astype(jnp.float32), axis=0),
            jnp.sum(grad_out, axis=0),
            grad_qbias[:inner],
            grad_qbias[2 * inner :],
            jnp.sum(grad_pre.astype(jnp.float32), axis=0),
        ]
    ).reshape(-1, 128)
    sum_qkv, sum_proj, sum_up, sum_down, all_small = ring_scatter(
        [
            turned(normed_low, grad_low_qkv),
            turned(grad_attn, context_low),
            turned(normed_mid, grad_pre),
            turned(grad_low, hidden_low),
        ],
        small,
        groups,
        7,
    )
    sums = jnp.sum(all_small, axis=0).reshape(-1)
    ends = 6 * width
    sum_vectors = lax.dynamic_slice_in_dim(
        sums[:ends].reshape(6, width), device * share, share, 1
    )
    sum_qbias = sums[ends : ends + 2 * inner].reshape(2, inner)
    sum_upbias = sums[ends + 2 * inner :]
    qkv_new = adamw(
        qkv_weight, sum_qkv.reshape(share, 3, inner), qkv_first, qkv_second, 0.1, 0.1
    )
    proj_new = adamw(proj_weight, sum_proj.T, proj_first, proj_second, 1.0, 0.1)
    up_new = adamw(up_weight, sum_up, up_first, up_second, 0.1, 0.1)
    down_new = adamw(down_weight, sum_down.T, down_first, down_second, 0.05, 0.1)
    qbias_new = adamw(qkv_bias, sum_qbias, qbias_first, qbias_second, 1.0, 0.0)
    ubias_new = adamw(up_bias, sum_upbias, ubias_first, ubias_second, 1.0, 0.0)
    vector_new = adamw(layer_vectors, sum_vectors, vector_first, vector_second, 1.0, 0.0)
    return (
        block_output.reshape(seqs, rows, width),
        input_grad.reshape(seqs, rows, width),
        *qkv_new,
        *proj_new,
        *up_new,
        *down_new,
        *qbias_new,
        *ubias_new,
        *vector_new,
    )


def solution(mesh):
    groups = mesh.shape["ctx"]
    tiled = groups % 4 == 0 and WIDTH % (groups * 16) == 0
    return jax.shard_map(
        ring_local if tiled else local,
        mesh=mesh,
        in_specs=(
            P(None, "ctx", None),
            P(None, "ctx", None),
            P(),
            P("ctx", None, "tp"),
            P("tp", "ctx"),
            P("ctx", "tp"),
            P("tp", "ctx"),
            P(None, "tp"),
            P("tp"),
            P(None, "ctx"),
            P("ctx", None, "tp"),
            P("ctx", None, "tp"),
            P("tp", "ctx"),
            P("tp", "ctx"),
            P("ctx", "tp"),
            P("ctx", "tp"),
            P("tp", "ctx"),
            P("tp", "ctx"),
            P(None, "tp"),
            P(None, "tp"),
            P("tp"),
            P("tp"),
            P(None, "ctx"),
            P(None, "ctx"),
        ),
        out_specs=(
            P(None, "ctx", None),
            P(None, "ctx", None),
            P("ctx", None, "tp"),
            P("ctx", None, "tp"),
            P("ctx", None, "tp"),
            P("tp", "ctx"),
            P("tp", "ctx"),
            P("tp", "ctx"),
            P("ctx", "tp"),
            P("ctx", "tp"),
            P("ctx", "tp"),
            P("tp", "ctx"),
            P("tp", "ctx"),
            P("tp", "ctx"),
            P(None, "tp"),
            P(None, "tp"),
            P(None, "tp"),
            P("tp"),
            P("tp"),
            P("tp"),
            P(None, "ctx"),
            P(None, "ctx"),
            P(None, "ctx"),
        ),
        check_vma=False,
    )
```

```python
from functools import partial
import math

import jax
import jax.numpy as jnp
from jax import lax
from jax.experimental import pallas as pl
from jax.experimental.pallas import tpu as pltpu
from jax.sharding import PartitionSpec as P

HD = 64
STEP = 10
WIDTH = 768
MESH = pl.DeviceIdType.MESH
VMEM_LIMIT = 48 * 1024 * 1024


BETA_ONE = 0.9
BETA_TWO = 0.95
EPSILON = 1e-08


def layer_norm(values, gain, shift):
    center = values - jnp.mean(values, axis=-1, keepdims=True)
    spread = jnp.mean(center * center, axis=-1, keepdims=True)
    return center * lax.rsqrt(spread + 1e-05) * gain + shift


def gelu_tanh(values):
    return (
        0.5
        * values
        * (1.0 + jnp.tanh(0.7978845608028654 * (values + 0.044715 * values * values * values)))
    )


def adamw(weight, grad, first, second, rate, decay):
    first_new = BETA_ONE * first + (1.0 - BETA_ONE) * grad
    second_new = BETA_TWO * second + (1.0 - BETA_TWO) * grad * grad
    first_hat = first_new / (1.0 - BETA_ONE**STEP)
    second_hat = second_new / (1.0 - BETA_TWO**STEP)
    weight_new = weight - rate * (first_hat / (jnp.sqrt(second_hat) + EPSILON) + decay * weight)
    return (weight_new, first_new, second_new)


def block_positions(order, start, count, blk):
    blocks = lax.dynamic_slice_in_dim(order, start // blk, count // blk, 1)
    offsets = jnp.arange(blk, dtype=jnp.int32)
    return (blocks[:, :, None] * blk + offsets[None, None, :]).reshape(order.shape[0], count)


def row_blocks(array, size):
    shape = array.shape
    return jnp.moveaxis(array.reshape((shape[0], shape[1] // size, size) + shape[2:]), 1, 0)


def forward_fold(carry, piece, start, queries, query_pos, order, blk):
    key_rows, value_rows = piece
    seqs, count, width = key_rows.shape
    heads = width // HD
    size = math.gcd(count, 512)
    key_pos = block_positions(order, start, count, blk)

    def step(state, block):
        key_block, value_block, place_block = block
        running_max, running_sum, context_sum = state
        key_heads = key_block.reshape(seqs, size, heads, HD)
        value_heads = value_block.reshape(seqs, size, heads, HD)
        scores = (
            jnp.einsum("sqhd,skhd->shqk", queries, key_heads, preferred_element_type=jnp.float32)
            * 0.125
        )
        allowed = query_pos[:, None, :, None] >= place_block[:, None, None, :]
        scores = jnp.where(allowed, scores, -1000000000.0)
        top_now = jnp.maximum(running_max, jnp.max(scores, axis=-1))
        rescale = jnp.exp(running_max - top_now)
        shares = jnp.exp(scores - top_now[..., None])
        running_sum = running_sum * rescale + jnp.sum(shares, axis=-1)
        context_sum = context_sum * rescale[..., None] + jnp.einsum(
            "shqk,skhd->shqd",
            shares.astype(jnp.bfloat16),
            value_heads,
            preferred_element_type=jnp.float32,
        )
        return ((top_now, running_sum, context_sum), None)

    carry, _ = lax.scan(
        step,
        carry,
        (row_blocks(key_rows, size), row_blocks(value_rows, size), row_blocks(key_pos, size)),
    )
    return carry


def keeping_fold(carry, piece, start, forward_step):
    state, key_store, value_store = carry
    key_rows, value_rows = piece
    key_store = key_rows
    value_store = value_rows
    state = forward_step(state, piece, start)
    return (state, key_store, value_store)


def query_fold(carry, piece, start, queries, grad_heads, log_total, delta, query_pos, order, blk):
    key_rows, value_rows = piece
    seqs, count, width = key_rows.shape
    heads = width // HD
    size = math.gcd(count, 512)
    key_pos = block_positions(order, start, count, blk)

    def step(grad_sum, block):
        key_block, value_block, place_block = block
        key_heads = key_block.reshape(seqs, size, heads, HD)
        value_heads = value_block.reshape(seqs, size, heads, HD)
        scores = (
            jnp.einsum("sqhd,skhd->shqk", queries, key_heads, preferred_element_type=jnp.float32)
            * 0.125
        )
        allowed = query_pos[:, None, :, None] >= place_block[:, None, None, :]
        scores = jnp.where(allowed, scores, -1000000000.0)
        shares = jnp.exp(scores - log_total[..., None])
        grad_share = jnp.einsum(
            "sqhd,skhd->shqk", grad_heads, value_heads, preferred_element_type=jnp.float32
        )
        grad_score = shares * (grad_share - delta[..., None])
        grad_sum = (
            grad_sum
            + jnp.einsum(
                "shqk,skhd->shqd",
                grad_score.astype(jnp.bfloat16),
                key_heads,
                preferred_element_type=jnp.float32,
            )
            * 0.125
        )
        return (grad_sum, None)

    carry, _ = lax.scan(
        step,
        carry,
        (row_blocks(key_rows, size), row_blocks(value_rows, size), row_blocks(key_pos, size)),
    )
    return carry


def key_fold(carry, piece, start, key_heads, value_heads, key_pos, order, blk):
    query_rows, grad_rows, log_rows, delta_rows = piece
    seqs, count, width = query_rows.shape
    heads = width // HD
    size = math.gcd(count, 512)
    query_pos = block_positions(order, start, count, blk)

    def step(state, block):
        grad_keys, grad_values = state
        query_block, grad_block, log_block, delta_block, place_block = block
        query_heads = query_block.reshape(seqs, size, heads, HD)
        grad_heads = grad_block.reshape(seqs, size, heads, HD)
        log_heads = jnp.transpose(log_block, (0, 2, 1))
        delta_heads = jnp.transpose(delta_block, (0, 2, 1))
        scores = (
            jnp.einsum(
                "sihd,sjhd->shij", query_heads, key_heads, preferred_element_type=jnp.float32
            )
            * 0.125
        )
        allowed = place_block[:, None, :, None] >= key_pos[:, None, None, :]
        scores = jnp.where(allowed, scores, -1000000000.0)
        shares = jnp.exp(scores - log_heads[..., None])
        grad_values = grad_values + jnp.einsum(
            "shij,sihd->shjd",
            shares.astype(jnp.bfloat16),
            grad_heads,
            preferred_element_type=jnp.float32,
        )
        grad_share = jnp.einsum(
            "sihd,sjhd->shij", grad_heads, value_heads, preferred_element_type=jnp.float32
        )
        grad_score = shares * (grad_share - delta_heads[..., None])
        grad_keys = (
            grad_keys
            + jnp.einsum(
                "shij,sihd->shjd",
                grad_score.astype(jnp.bfloat16),
                query_heads,
                preferred_element_type=jnp.float32,
            )
            * 0.125
        )
        return ((grad_keys, grad_values), None)

    carry, _ = lax.scan(
        step,
        carry,
        (
            row_blocks(query_rows, size),
            row_blocks(grad_rows, size),
            row_blocks(log_rows, size),
            row_blocks(delta_rows, size),
            row_blocks(query_pos, size),
        ),
    )
    return carry


def local(
    tokens,
    out_grad,
    block_order,
    qkv_weight,
    proj_weight,
    up_weight,
    down_weight,
    qkv_bias,
    up_bias,
    layer_vectors,
    qkv_first,
    qkv_second,
    proj_first,
    proj_second,
    up_first,
    up_second,
    down_first,
    down_second,
    qbias_first,
    qbias_second,
    ubias_first,
    ubias_second,
    vector_first,
    vector_second,
):
    device = lax.axis_index("ctx")
    groups = lax.axis_size("ctx")
    seqs, rows, width = tokens.shape
    blk = rows // 2
    query_pos = block_positions(block_order, device * rows, rows, blk)
    qkv_full, up_full, proj_full, down_full = (
        lax.all_gather(qkv_weight.astype(jnp.bfloat16), "ctx", axis=0, tiled=True),
        lax.all_gather(up_weight.astype(jnp.bfloat16), "ctx", axis=0, tiled=True),
        lax.all_gather(proj_weight.astype(jnp.bfloat16), "ctx", axis=1, tiled=True),
        lax.all_gather(down_weight.astype(jnp.bfloat16), "ctx", axis=1, tiled=True),
    )
    layer_vector_rows = lax.all_gather(layer_vectors, "ctx", axis=1, tiled=True)
    inputs = tokens.astype(jnp.float32)
    first_normalized, norm_one_back = jax.vjp(
        layer_norm, inputs, layer_vector_rows[0], layer_vector_rows[1]
    )
    normed_low = first_normalized.astype(jnp.bfloat16)
    projection_output = jnp.einsum(
        "sqd,dcf->sqcf", normed_low, qkv_full, preferred_element_type=jnp.float32
    )
    queries = (projection_output[:, :, 0] + qkv_bias[0]).astype(jnp.bfloat16)
    keys = projection_output[:, :, 1].astype(jnp.bfloat16)
    values = (projection_output[:, :, 2] + qkv_bias[1]).astype(jnp.bfloat16)
    heads = queries.shape[-1] // HD
    query_heads = queries.reshape(seqs, rows, heads, HD)
    key_heads = keys.reshape(seqs, rows, heads, HD)
    value_heads = values.reshape(seqs, rows, heads, HD)
    start_state = (
        jnp.full((seqs, heads, rows), -1e30, jnp.float32),
        jnp.zeros((seqs, heads, rows), jnp.float32),
        jnp.zeros((seqs, heads, rows, HD), jnp.float32),
    )
    forward_step = partial(
        forward_fold, queries=query_heads, query_pos=query_pos, order=block_order, blk=blk
    )
    empty_store = jnp.zeros((seqs, rows * groups, keys.shape[-1]), jnp.bfloat16)
    folded, key_store, value_store = keeping_fold(
        (start_state, empty_store, empty_store),
        (
            lax.all_gather(keys, "ctx", axis=1, tiled=True),
            lax.all_gather(values, "ctx", axis=1, tiled=True),
        ),
        jnp.int32(0),
        forward_step=forward_step,
    )
    running_max, running_sum, context_sum = folded
    whole_pair = (key_store, value_store)
    log_total = running_max + jnp.log(running_sum)
    context_value = context_sum / running_sum[..., None]
    context_rows = jnp.transpose(context_value, (0, 2, 1, 3)).reshape(seqs, rows, heads * HD)
    context_low = context_rows.astype(jnp.bfloat16)
    attn_part = jnp.einsum(
        "sqf,fd->sqd", context_low, proj_full, preferred_element_type=jnp.float32
    )
    attention_result = lax.psum(attn_part, "tp") + layer_vector_rows[4]
    middle = inputs + attention_result
    second_normalized, norm_two_back = jax.vjp(
        layer_norm, middle, layer_vector_rows[2], layer_vector_rows[3]
    )
    normed_mid = second_normalized.astype(jnp.bfloat16)
    hidden_preactivation = (
        jnp.einsum("sqd,df->sqf", normed_mid, up_full, preferred_element_type=jnp.float32) + up_bias
    )
    hidden_activation, gelu_back = jax.vjp(gelu_tanh, hidden_preactivation)
    hidden_low = hidden_activation.astype(jnp.bfloat16)
    mlp_part = jnp.einsum("sqf,fd->sqd", hidden_low, down_full, preferred_element_type=jnp.float32)
    mlp_total = lax.psum(mlp_part, "tp") + layer_vector_rows[5]
    block_output = (middle + mlp_total).astype(jnp.bfloat16)
    grad_out = out_grad.astype(jnp.float32)
    grad_down = jnp.einsum("sqf,sqd->fd", hidden_low, out_grad, preferred_element_type=jnp.float32)
    grad_hidden = jnp.einsum("sqd,fd->sqf", out_grad, down_full, preferred_element_type=jnp.float32)
    grad_pre = gelu_back(grad_hidden)[0].astype(jnp.bfloat16)
    grad_up = jnp.einsum("sqd,sqf->df", normed_mid, grad_pre, preferred_element_type=jnp.float32)
    grad_upbias = jnp.sum(grad_pre.astype(jnp.float32), axis=(0, 1))
    mid_part = jnp.einsum("sqf,df->sqd", grad_pre, up_full, preferred_element_type=jnp.float32)
    grad_normed_two = lax.psum(mid_part, "tp")
    grad_mid_norm, grad_gain_two, grad_shift_two = norm_two_back(grad_normed_two)
    grad_middle = grad_out + grad_mid_norm
    grad_attn = grad_middle.astype(jnp.bfloat16)
    grad_proj = jnp.einsum(
        "sqf,sqd->fd", context_low, grad_attn, preferred_element_type=jnp.float32
    )
    grad_context = jnp.einsum(
        "sqd,fd->sqf", grad_attn, proj_full, preferred_element_type=jnp.float32
    ).astype(jnp.bfloat16)
    grad_heads = grad_context.reshape(seqs, rows, heads, HD)
    row_delta = jnp.sum(
        grad_heads.astype(jnp.float32) * context_rows.reshape(seqs, rows, heads, HD), axis=-1
    )
    delta_heads = jnp.transpose(row_delta, (0, 2, 1))
    log_rows = jnp.transpose(log_total, (0, 2, 1))
    zero_heads = jnp.zeros((seqs, heads, rows, HD), jnp.float32)
    query_step = partial(
        query_fold,
        queries=query_heads,
        grad_heads=grad_heads,
        log_total=log_total,
        delta=delta_heads,
        query_pos=query_pos,
        order=block_order,
        blk=blk,
    )
    grad_q_sum = query_step(zero_heads, whole_pair, 0)
    key_step = partial(
        key_fold,
        key_heads=key_heads,
        value_heads=value_heads,
        key_pos=query_pos,
        order=block_order,
        blk=blk,
    )
    grad_k_sum, grad_v_sum = key_step(
        (zero_heads, zero_heads),
        (
            lax.all_gather(queries.astype(jnp.float32), "ctx", axis=1, tiled=True).astype(
                jnp.bfloat16
            ),
            lax.all_gather(grad_context.astype(jnp.float32), "ctx", axis=1, tiled=True).astype(
                jnp.bfloat16
            ),
            lax.all_gather(log_rows, "ctx", axis=1, tiled=True),
            lax.all_gather(row_delta, "ctx", axis=1, tiled=True),
        ),
        jnp.int32(0),
    )

    def head_rows(array):
        return (
            jnp.transpose(array, (0, 2, 1, 3)).reshape(seqs, rows, heads * HD).astype(jnp.bfloat16)
        )

    grad_qkv_low = jnp.stack(
        [head_rows(grad_q_sum), head_rows(grad_k_sum), head_rows(grad_v_sum)], axis=2
    )
    grad_qkv = jnp.einsum(
        "sqd,sqcf->dcf", normed_low, grad_qkv_low, preferred_element_type=jnp.float32
    )
    grad_qbias = jnp.sum(grad_qkv_low[:, :, 0::2].astype(jnp.float32), axis=(0, 1))
    first_part = jnp.einsum(
        "sqcf,dcf->sqd", grad_qkv_low, qkv_full, preferred_element_type=jnp.float32
    )
    grad_normed_one = lax.psum(first_part, "tp")
    grad_in_norm, grad_gain_one, grad_shift_one = norm_one_back(grad_normed_one)
    input_grad = grad_middle + grad_in_norm
    grad_vectors = jnp.stack(
        [
            grad_gain_one,
            grad_shift_one,
            grad_gain_two,
            grad_shift_two,
            jnp.sum(grad_attn.astype(jnp.float32), axis=(0, 1)),
            jnp.sum(grad_out, axis=(0, 1)),
        ]
    )
    sum_qkv, sum_up, sum_proj, sum_down, sum_vectors = (
        lax.psum_scatter(grad_qkv, "ctx", scatter_dimension=0, tiled=True),
        lax.psum_scatter(grad_up, "ctx", scatter_dimension=0, tiled=True),
        lax.psum_scatter(grad_proj, "ctx", scatter_dimension=1, tiled=True),
        lax.psum_scatter(grad_down, "ctx", scatter_dimension=1, tiled=True),
        lax.psum_scatter(grad_vectors, "ctx", scatter_dimension=1, tiled=True),
    )
    sum_qbias, sum_upbias = lax.psum((grad_qbias, grad_upbias), "ctx")
    qkv_new = adamw(qkv_weight, sum_qkv, qkv_first, qkv_second, 0.1, 0.1)
    proj_new = adamw(proj_weight, sum_proj, proj_first, proj_second, 1.0, 0.1)
    up_new = adamw(up_weight, sum_up, up_first, up_second, 0.1, 0.1)
    down_new = adamw(down_weight, sum_down, down_first, down_second, 0.05, 0.1)
    qbias_new = adamw(qkv_bias, sum_qbias, qbias_first, qbias_second, 1.0, 0.0)
    ubias_new = adamw(up_bias, sum_upbias, ubias_first, ubias_second, 1.0, 0.0)
    vector_new = adamw(layer_vectors, sum_vectors, vector_first, vector_second, 1.0, 0.0)
    return (
        block_output,
        input_grad,
        qkv_new[0],
        qkv_new[1],
        qkv_new[2],
        proj_new[0],
        proj_new[1],
        proj_new[2],
        up_new[0],
        up_new[1],
        up_new[2],
        down_new[0],
        down_new[1],
        down_new[2],
        qbias_new[0],
        qbias_new[1],
        qbias_new[2],
        ubias_new[0],
        ubias_new[1],
        ubias_new[2],
        vector_new[0],
        vector_new[1],
        vector_new[2],
    )


def chip_at(place, chips):
    half = chips // 2
    back = place // half
    return (1 - back) * 2 * place + back * (2 * (chips - 1 - place) + 1)


class Ring:
    def __init__(self, chips):
        me = lax.axis_index("ctx")
        self.chips, self.me = chips, me
        self.core = me % 2
        chip = me // 2
        along, across = chip // 2, chip % 2
        self.place = along + across * (chips - 1 - 2 * along)
        self.right, self.left = self.slot(1), self.slot(-1)
        self.mate = chip * 2 + 1 - self.core

    def slot(self, ahead, other=False):
        place = (self.place + ahead + 2 * self.chips) % self.chips
        core = 1 - self.core if other else self.core
        return chip_at(place, self.chips) * 2 + core

    def greet(self, count=3):
        barrier = pltpu.get_barrier_semaphore()
        for device in (self.left, self.right, self.mate):
            pl.semaphore_signal(barrier, inc=1, device_id={"ctx": device}, device_id_type=MESH)
        pl.semaphore_wait(barrier, count)


def remote(src, dst, send, recv, device):
    return pltpu.make_async_remote_copy(
        src_ref=src,
        dst_ref=dst,
        send_sem=send,
        recv_sem=recv,
        device_id={"ctx": device},
        device_id_type=MESH,
    )


class Gather:
    def __init__(self, ring, ins, outs, sems):
        self.ring, self.ins, self.outs = ring, ins, outs
        self.ring_send, self.ring_recv, self.mate_send, self.mate_recv, self.own = sems
        self.far_right = ring.chips // 2
        self.far_left = ring.chips - 1 - self.far_right
        self.sent = []

    def hop(self, at, src, slot, index, device):
        copy = remote(
            src, self.outs[at].at[slot], self.ring_send.at[at, index],
            self.ring_recv.at[at, index], device,
        )
        return copy

    def pass_on(self, at, src, slot, index):
        copy = remote(
            src, self.outs[at].at[slot], self.mate_send.at[at, index],
            self.mate_recv.at[at, index], self.ring.mate,
        )
        return copy

    def go(self, copy):
        copy.start()
        self.sent.append(copy)

    def start(self):
        ring = self.ring
        for at, block in enumerate(self.ins):
            self.go(self.hop(at, block, ring.me, 0, ring.right))
            self.go(self.hop(at, block, ring.me, self.far_right, ring.left))
            self.go(self.pass_on(at, block, ring.me, 0))
            pltpu.make_async_copy(block, self.outs[at].at[ring.me], self.own.at[at]).start()

    def step(self, step):
        ring = self.ring
        for at in range(len(self.ins)):
            for sign, far, base, device in (
                (-1, self.far_right, 0, ring.right),
                (1, self.far_left, self.far_right, ring.left),
            ):
                if step >= far:
                    continue
                slot = ring.slot(sign * (step + 1))
                block = self.outs[at].at[slot]
                self.hop(at, block, slot, base + step, device).wait_recv()
                if step + 1 < far:
                    self.go(self.hop(at, block, slot, base + step + 1, device))
                self.go(self.pass_on(at, block, slot, 1 + base + step))

    def finish(self):
        ring = self.ring
        for at in range(len(self.ins)):
            order = [0] + [-(s + 1) for s in range(self.far_right)]
            order += [s + 1 for s in range(self.far_left)]
            for index, ahead in enumerate(order):
                slot = ring.slot(ahead, other=True)
                self.pass_on(at, self.outs[at].at[slot], slot, index).wait_recv()
            pltpu.make_async_copy(
                self.ins[at], self.outs[at].at[ring.me], self.own.at[at]
            ).wait()
        for copy in self.sent:
            copy.wait_send()


def gather_sems(count, chips):
    return [pltpu.SemaphoreType.DMA((count, chips))] * 4 + [pltpu.SemaphoreType.DMA((count,))]


class Scatter:
    def __init__(self, ring, pieces, grads, mates, lands, outs, sems):
        self.ring, self.pieces = ring, pieces
        self.grads, self.mates, self.lands, self.outs = grads, mates, lands, outs
        self.mate_send, self.mate_recv, self.ring_send, self.ring_recv = sems
        self.order = []
        for far in range(1, ring.chips // 2):
            self.order += [-far, far]
        self.order += [ring.chips // 2, 0]
        self.arrived = set()
        self.sent = []

    def to_mate(self, index, at):
        ring = self.ring
        return remote(
            self.grads[at].at[ring.slot(self.order[index], other=True)],
            self.mates[at].at[index],
            self.mate_send.at[at, index], self.mate_recv.at[at, index], ring.mate,
        )

    def start(self):
        for index in range(self.ring.chips):
            for at in range(len(self.grads)):
                copy = self.to_mate(index, at)
                copy.start()
                self.sent.append(copy)

    def own_part(self, ahead, at, columns):
        half = self.ring.chips // 2 - 1
        ahead = (ahead + half) % self.ring.chips - half
        index = self.order.index(ahead)
        if (index, at) not in self.arrived:
            self.arrived.add((index, at))
            self.to_mate(index, at).wait_recv()
        mine = self.grads[at][self.ring.slot(ahead), :, columns].astype(jnp.float32)
        return mine + self.mates[at][index, :, columns].astype(jnp.float32)

    def hop(self, which, step, src):
        device = self.ring.right if self.pieces[which][3] > 0 else self.ring.left
        return remote(
            src, self.lands[which].at[step], self.ring_send.at[which, step],
            self.ring_recv.at[which, step], device,
        )

    def step(self, step):
        chips = self.ring.chips
        for which, (at, first, count, sign) in enumerate(self.pieces):
            columns = slice(first, first + count)
            land = self.lands[which]
            part = self.own_part(-sign * (step + 1), at, columns)
            if step > 0:
                self.hop(which, step - 1, land.at[step - 1]).wait_recv()
                part = part + land[step - 1].astype(jnp.float32)
            if step < chips - 1:
                hold = land.at[chips - 1 + step]
                hold[...] = part.astype(jnp.bfloat16)
                copy = self.hop(which, step, hold)
                copy.start()
                self.sent.append(copy)
            else:
                self.outs[at][:, columns] = part

    def finish(self):
        for copy in self.sent:
            copy.wait_send()


def scatter_scratch(blocks, pieces, chips):
    rows, dma = blocks[0].shape[1], pltpu.SemaphoreType.DMA
    return (
        [pltpu.VMEM((chips, rows, b.shape[2]), jnp.bfloat16) for b in blocks]
        + [pltpu.VMEM((2 * chips - 2, rows, p[2]), jnp.bfloat16) for p in pieces]
        + [dma((len(blocks), chips))] * 2
        + [dma((len(pieces), chips))] * 2
    )


def row_split(array, groups):
    return array.reshape(groups, array.shape[0] // groups, array.shape[1])


def tail_kernel(chips, pieces, *refs):
    grad, part, normal, small_in = refs[0:4]
    out, total, small_out = refs[4:7]
    hold, land, small, mate = refs[7:11]
    lands, sems = refs[11 : 11 + len(pieces)], refs[11 + len(pieces) :]
    pair_send, pair_recv = sems[4:6]
    other = 1 - lax.axis_index("tp")
    ring = Ring(chips)
    barrier = pltpu.get_barrier_semaphore()
    pl.semaphore_signal(barrier, inc=1, device_id={"tp": other}, device_id_type=MESH)
    ring.greet(4)
    scatter = Scatter(ring, pieces, [grad], [mate], lands, [out], sems[:4])
    scatter.start()
    hold[...] = part[...].astype(jnp.bfloat16)
    pair = pltpu.make_async_remote_copy(
        src_ref=hold, dst_ref=land, send_sem=pair_send.at[0], recv_sem=pair_recv.at[0],
        device_id={"tp": other}, device_id_type=MESH,
    )
    pair.start()
    gather = Gather(ring, [small], [small_out], sems[6:])
    scatter.step(0)
    scatter.step(1)
    small[...] = small_in[...]
    pair.wait()
    summed = hold[...].astype(jnp.float32) + land[...].astype(jnp.float32)
    total[...] = summed
    small[0:1, :] = jnp.sum(summed * normal[...], axis=0, keepdims=True)
    small[1:2, :] = jnp.sum(summed, axis=0, keepdims=True)
    gather.start()
    for step in range(2, chips):
        scatter.step(step)
        if step - 2 < gather.far_right:
            gather.step(step - 2)
    gather.finish()
    scatter.finish()


def tail(grad, part, normal, small, groups, collective):
    chips = groups // 2
    block = row_split(grad, groups)
    columns = block.shape[2]
    right = columns // 256 * 128
    pieces = ((0, 0, right, 1), (0, right, columns - right, -1))
    vmem = pl.BlockSpec(memory_space=pltpu.VMEM)
    dma = pltpu.SemaphoreType.DMA
    return pl.pallas_call(
        partial(tail_kernel, chips, pieces),
        out_shape=[
            jax.ShapeDtypeStruct(block.shape[1:], jnp.float32),
            jax.ShapeDtypeStruct(part.shape, jnp.float32),
            jax.ShapeDtypeStruct((groups,) + small.shape, jnp.float32),
        ],
        in_specs=[vmem] * 4,
        out_specs=[vmem] * 3,
        scratch_shapes=[pltpu.VMEM(part.shape, jnp.bfloat16)] * 2
        + [pltpu.VMEM(small.shape, jnp.float32)]
        + scatter_scratch([block], pieces, chips)
        + [dma((1,)), dma((1,))]
        + gather_sems(1, chips),
        compiler_params=pltpu.CompilerParams(
            collective_id=collective, has_side_effects=True, vmem_limit_bytes=VMEM_LIMIT
        ),
    )(block, part, normal, small)


def pair_kernel(count, *refs):
    ins, outs = refs[:count], refs[count : 2 * count]
    holds, lands = refs[2 * count : 3 * count], refs[3 * count : 4 * count]
    send, recv = refs[4 * count :]
    other = 1 - lax.axis_index("tp")
    barrier = pltpu.get_barrier_semaphore()
    pl.semaphore_signal(barrier, inc=1, device_id={"tp": other}, device_id_type=MESH)
    for at in range(count):
        holds[at][...] = ins[at][...].astype(jnp.bfloat16)
    pl.semaphore_wait(barrier, 1)
    copies = []
    for at in range(count):
        copy = pltpu.make_async_remote_copy(
            src_ref=holds[at], dst_ref=lands[at], send_sem=send.at[at], recv_sem=recv.at[at],
            device_id={"tp": other}, device_id_type=MESH,
        )
        copy.start()
        copies.append(copy)
    for at in range(count):
        copies[at].wait()
        outs[at][...] = holds[at][...].astype(jnp.float32) + lands[at][...].astype(jnp.float32)


def pair_sum(arrays, collective):
    count = len(arrays)
    vmem = pl.BlockSpec(memory_space=pltpu.VMEM)
    return pl.pallas_call(
        partial(pair_kernel, count),
        out_shape=[jax.ShapeDtypeStruct(a.shape, jnp.float32) for a in arrays],
        in_specs=[vmem] * count,
        out_specs=[vmem] * count,
        scratch_shapes=[pltpu.VMEM(a.shape, jnp.bfloat16) for a in arrays] * 2
        + [pltpu.SemaphoreType.DMA((count,))] * 2,
        compiler_params=pltpu.CompilerParams(
            collective_id=collective, has_side_effects=True, vmem_limit_bytes=VMEM_LIMIT
        ),
    )(*arrays)


NT = (((1,), (1,)), ((), ()))
NN = (((1,), (0,)), ((), ()))


def mul(left, right, dims):
    return lax.dot_general(left, right, dims, preferred_element_type=jnp.float32)


def attend_unit(heads, seq, head, rows, allowed, own, every, context_ref):
    width = heads * HD
    here = slice(seq * rows, (seq + 1) * rows)
    at = slice(head * HD, (head + 1) * HD)
    keys = every[:, here, width + head * HD : width + (head + 1) * HD].reshape(-1, HD)
    values = every[:, here, 2 * width + head * HD : 2 * width + (head + 1) * HD].reshape(-1, HD)
    scores = mul(own(here, at), keys, NT) * 0.125
    scores = jnp.where(allowed, scores, -1000000000.0)
    top = jnp.max(scores, axis=-1, keepdims=True)
    shares = jnp.exp(scores - top)
    total = jnp.sum(shares, axis=-1, keepdims=True)
    mixed = mul(shares.astype(jnp.bfloat16), values, NN)
    context_ref[here, at] = mixed / total
    return top + jnp.log(total)


def front_kernel(chips, heads, *refs):
    ins, (bias, own_pos, all_pos) = refs[0:5], refs[5:8]
    outs, vectors_ref, every, context_ref, log_ref = refs[8:13], *refs[13:17]
    tokens_all, sems = outs[1], refs[17:]
    width = heads * HD
    groups = 2 * chips
    seqs = own_pos.shape[0]
    rows = tokens_all.shape[1] // seqs
    ring = Ring(chips)
    ring.greet()
    first = Gather(ring, ins[0:2], outs[0:2], sems[0:5])
    second = Gather(ring, ins[2:5], outs[2:5], sems[5:10])
    first.start()
    for step in range(first.far_right - 1):
        first.step(step)
    second.start()
    first.step(first.far_right - 1)
    first.finish()
    packed = outs[0]
    extra = packed[:, :, 3 * width :].reshape(-1, 128).astype(jnp.float32).T
    vectors = (extra[0:6] + extra[6:12]) + extra[12:18]
    vectors_ref[0:6, :] = vectors
    gain, shift = vectors[0:1], vectors[1:2]

    def project(at, carry):
        values = tokens_all[pl.ds(2 * at, 2)].reshape(-1, tokens_all.shape[2])
        normed = layer_norm(values.astype(jnp.float32), gain, shift).astype(jnp.bfloat16)
        weights = packed[:, :, : 3 * width].reshape(-1, 3 * width)
        result = (mul(normed, weights, NN) + bias[...]).astype(jnp.bfloat16)
        every[pl.ds(2 * at, 2)] = result.reshape(2, -1, 3 * width)
        return carry

    lax.fori_loop(0, groups // 4, project, 0)
    second.step(0)
    lax.fori_loop(groups // 4, groups // 2, project, 0)
    second.step(1)

    def own(here, at):
        return every[ring.me, here, at]

    lanes = lax.broadcasted_iota(jnp.int32, (rows, 128), 1)
    for seq in range(seqs):
        allowed = own_pos[seq] >= all_pos[seq]
        logs = jnp.zeros((rows, 128), jnp.float32)
        for head in range(heads):
            log = attend_unit(heads, seq, head, rows, allowed, own, every, context_ref)
            logs = jnp.where(lanes == head, log, logs)
        log_ref[seq * rows : (seq + 1) * rows, :] = logs
        if seq + 2 < second.far_right:
            second.step(seq + 2)
    for step in range(seqs + 2, second.far_right):
        second.step(step)
    second.finish()


def front(arrays, bias, own_pos, all_pos, heads, groups, collective):
    vmem = pl.BlockSpec(memory_space=pltpu.VMEM)
    hbm = pl.BlockSpec(memory_space=pl.ANY)
    many, width = arrays[1].shape
    chips = groups // 2
    return pl.pallas_call(
        partial(front_kernel, chips, heads),
        out_shape=[jax.ShapeDtypeStruct((groups,) + a.shape, a.dtype) for a in arrays]
        + [
            jax.ShapeDtypeStruct((8, width), jnp.float32),
            jax.ShapeDtypeStruct((groups, many, 3 * heads * HD), jnp.bfloat16),
            jax.ShapeDtypeStruct((many, heads * HD), jnp.float32),
            jax.ShapeDtypeStruct((many, 128), jnp.float32),
        ],
        in_specs=[vmem] * 2 + [hbm] * 3 + [vmem] * 3,
        out_specs=[vmem] * 2 + [hbm] * 3 + [vmem] * 4,
        scratch_shapes=gather_sems(2, chips) + gather_sems(3, chips),
        compiler_params=pltpu.CompilerParams(
            collective_id=collective, has_side_effects=True, vmem_limit_bytes=VMEM_LIMIT
        ),
    )(*arrays, bias, own_pos, all_pos)


def back_kernel(chips, heads, pieces, *refs):
    own, every, own_pos, all_pos = refs[0:4]
    grads, out_ref, sums = refs[4:7], refs[7], refs[8:11]
    gathered, mates, lands = refs[11], refs[12:15], refs[15 : 15 + len(pieces)]
    sems = refs[15 + len(pieces) :]
    seqs = own_pos.shape[0]
    rows = own.shape[0] // seqs
    width = heads * HD
    ring = Ring(chips)
    me = ring.me
    ring.greet()
    gather = Gather(ring, [own], [gathered], sems[4:])
    scatter = Scatter(ring, pieces, grads, mates, lands, sums, sems[:4])
    gather.start()
    scatter.start()
    for step in range(gather.far_right - 1):
        gather.step(step)
    scatter.step(0)
    gather.step(gather.far_right - 1)
    gather.finish()
    done = 1
    for seq in range(seqs):
        here = slice(seq * rows, (seq + 1) * rows)
        allowed = own_pos[seq] >= all_pos[seq]
        allowed_back = own_pos[seq] <= all_pos[seq]
        stats = gathered[:, here, width:].reshape(-1, 128).astype(jnp.float32).T
        turned = (stats[0:16] + stats[16:32]) + stats[32:48]
        parts = own[here, width:].astype(jnp.float32)
        stat = (parts[:, 0:16] + parts[:, 16:32]) + parts[:, 32:48]
        for head in range(heads):
            at = slice(head * HD, (head + 1) * HD)
            past = slice(width + head * HD, width + (head + 1) * HD)
            last = slice(2 * width + head * HD, 2 * width + (head + 1) * HD)
            queries = every[:, here, at].reshape(-1, HD)
            keys = every[:, here, past].reshape(-1, HD)
            values = every[:, here, last].reshape(-1, HD)
            grad_all = gathered[:, here, at].reshape(-1, HD)
            query, key, value = every[me, here, at], every[me, here, past], every[me, here, last]
            scores = jnp.where(allowed, mul(query, keys, NT) * 0.125, -1000000000.0)
            shares = jnp.exp(scores - stat[:, head : head + 1])
            grad_share = mul(own[here, at], values, NT)
            delta = stat[:, heads + head : heads + head + 1]
            grad_score = (shares * (grad_share - delta)).astype(jnp.bfloat16)
            out_ref[here, at] = (mul(grad_score, keys, NN) * 0.125).astype(jnp.bfloat16)
            scores = jnp.where(allowed_back, mul(key, queries, NT) * 0.125, -1000000000.0)
            shares = jnp.exp(scores - turned[head : head + 1])
            grad_value = mul(shares.astype(jnp.bfloat16), grad_all, NN)
            grad_share = mul(value, grad_all, NT)
            grad_score = shares * (grad_share - turned[heads + head : heads + head + 1])
            grad_key = mul(grad_score.astype(jnp.bfloat16), queries, NN) * 0.125
            out_ref[here, past] = grad_key.astype(jnp.bfloat16)
            out_ref[here, last] = grad_value.astype(jnp.bfloat16)
            if head % 2 == 1 and done < chips - 1:
                scatter.step(done)
                done += 1
    for step in range(done, chips):
        scatter.step(step)
    scatter.finish()


def back(own, every, own_pos, all_pos, grads, heads, groups, collective):
    vmem = pl.BlockSpec(memory_space=pltpu.VMEM)
    chips = groups // 2
    blocks = [row_split(g, groups) for g in grads]
    proj, up, down = [b.shape[2] for b in blocks]
    cut = proj * 2 // 3 // 128 * 128
    pieces = ((1, 0, up, 1), (2, 0, down, -1), (0, 0, cut, 1), (0, cut, proj - cut, -1))
    return pl.pallas_call(
        partial(back_kernel, chips, heads, pieces),
        out_shape=[jax.ShapeDtypeStruct((own.shape[0], 3 * heads * HD), jnp.bfloat16)]
        + [jax.ShapeDtypeStruct(b.shape[1:], jnp.float32) for b in blocks],
        in_specs=[vmem] * 7,
        out_specs=[vmem] * 4,
        scratch_shapes=[pltpu.VMEM((groups,) + own.shape, own.dtype)]
        + scatter_scratch(blocks, pieces, chips)
        + gather_sems(1, chips),
        compiler_params=pltpu.CompilerParams(
            collective_id=collective, has_side_effects=True, vmem_limit_bytes=VMEM_LIMIT
        ),
    )(own, every, own_pos, all_pos, *blocks)


def three_parts(array):
    high = lax.reduce_precision(array, 8, 7)
    rest = array - high
    middle = lax.reduce_precision(rest, 8, 7)
    return [part.astype(jnp.bfloat16) for part in (high, middle, rest - middle)]


def ring_local(
    tokens,
    out_grad,
    block_order,
    qkv_weight,
    proj_weight,
    up_weight,
    down_weight,
    qkv_bias,
    up_bias,
    layer_vectors,
    qkv_first,
    qkv_second,
    proj_first,
    proj_second,
    up_first,
    up_second,
    down_first,
    down_second,
    qbias_first,
    qbias_second,
    ubias_first,
    ubias_second,
    vector_first,
    vector_second,
):
    device = lax.axis_index("ctx")
    groups = lax.axis_size("ctx")
    seqs, rows, width = tokens.shape
    blk = rows // 2
    share = qkv_weight.shape[0]
    inner = qkv_weight.shape[2]
    heads = inner // HD
    many = seqs * rows
    own_pos = block_positions(block_order, device * rows, rows, blk)[:, :, None]
    all_pos = block_positions(block_order, 0, rows * groups, blk)[:, None, :]
    low = jnp.bfloat16
    vector_parts = jnp.concatenate(three_parts(layer_vectors.T), axis=1)
    packed = jnp.concatenate(
        [
            qkv_weight.astype(low).reshape(share, 3 * inner),
            jnp.pad(vector_parts, ((0, 0), (0, 128 - vector_parts.shape[1]))),
        ],
        axis=1,
    )
    bias = jnp.concatenate([qkv_bias[0], jnp.zeros_like(qkv_bias[0]), qkv_bias[1]])[None]
    grad_low = out_grad.reshape(many, width)
    packed_full, _, proj_full, up_full, down_full, vectors, every, context, logs = front(
        [
            packed,
            tokens.reshape(many, width),
            proj_weight.astype(low).T,
            up_weight.astype(low),
            down_weight.astype(low).T,
        ],
        bias,
        own_pos,
        all_pos,
        heads,
        groups,
        1,
    )
    packed_full = packed_full.reshape(width, -1)
    qkv_full = packed_full[:, : 3 * inner]
    proj_full = proj_full.reshape(width, -1)
    up_full = up_full.reshape(width, -1)
    down_full = down_full.reshape(width, -1)
    inputs = tokens.reshape(many, width).astype(jnp.float32)
    first_normalized, norm_one_back = jax.vjp(layer_norm, inputs, vectors[0], vectors[1])
    normed_low = first_normalized.astype(low)
    center = inputs - jnp.mean(inputs, axis=-1, keepdims=True)
    normal = center * lax.rsqrt(jnp.mean(center * center, axis=-1, keepdims=True) + 1e-05)
    context_low = context.astype(low)
    (attn,) = pair_sum([mul(context_low, proj_full, NT)], 3)
    middle = inputs + (attn + vectors[4])
    second_normalized, norm_two_back = jax.vjp(layer_norm, middle, vectors[2], vectors[3])
    normed_mid = second_normalized.astype(low)
    hidden_preactivation = mul(normed_mid, up_full, NN) + up_bias
    hidden_activation, gelu_back = jax.vjp(gelu_tanh, hidden_preactivation)
    hidden_low = hidden_activation.astype(low)
    grad_hidden = mul(grad_low, down_full, NN)
    grad_pre = gelu_back(grad_hidden)[0].astype(low)
    mlp, grad_normed_two = pair_sum(
        [mul(hidden_low, down_full, NT), mul(grad_pre, up_full, NT)], 4
    )
    block_output = (middle + (mlp + vectors[5])).astype(low)
    grad_out = grad_low.astype(jnp.float32)
    grad_mid_norm, grad_gain_two, grad_shift_two = norm_two_back(grad_normed_two)
    grad_middle = grad_out + grad_mid_norm
    grad_attn = grad_middle.astype(low)
    grad_context = mul(grad_attn, proj_full, NN).astype(low)
    lanes = jnp.arange(128)[None, :]
    choose = (lanes == heads + jnp.arange(inner)[:, None] // HD).astype(jnp.float32)
    delta = jnp.dot(
        grad_context.astype(jnp.float32) * context, choose, precision=lax.Precision.HIGHEST
    )
    stats = three_parts((logs + delta)[:, :16])
    own = jnp.concatenate([grad_context] + stats + [jnp.zeros((many, 80), low)], axis=1)

    def turned(left, right):
        return lax.dot_general(
            left, right, (((0,), (0,)), ((), ())), preferred_element_type=jnp.float32
        ).astype(low)

    grad_low_qkv, sum_proj, sum_up, sum_down = back(
        own,
        every,
        own_pos,
        all_pos,
        [
            turned(grad_attn, context_low),
            turned(normed_mid, grad_pre),
            turned(grad_low, hidden_low),
        ],
        heads,
        groups,
        5,
    )
    grad_qbias = jnp.sum(grad_low_qkv.astype(jnp.float32), axis=0)
    small = jnp.concatenate(
        [
            jnp.zeros((2 * width,), jnp.float32),
            grad_gain_two,
            grad_shift_two,
            jnp.sum(grad_attn.astype(jnp.float32), axis=0),
            jnp.sum(grad_out, axis=0),
            grad_qbias[:inner],
            grad_qbias[2 * inner :],
            jnp.sum(grad_pre.astype(jnp.float32), axis=0),
        ]
    )
    used = small.shape[0]
    small = jnp.pad(small, (0, -used % (8 * width))).reshape(-1, width)
    sum_qkv, grad_normed_one, all_small = tail(
        turned(normed_low, grad_low_qkv),
        mul(grad_low_qkv, qkv_full, NT),
        normal,
        small,
        groups,
        6,
    )
    grad_in_norm = norm_one_back(grad_normed_one)[0]
    input_grad = grad_middle + grad_in_norm
    sums = jnp.sum(all_small, axis=0).reshape(-1)
    ends = 6 * width
    sum_vectors = lax.dynamic_slice_in_dim(
        sums[:ends].reshape(6, width), device * share, share, 1
    )
    sum_qbias = sums[ends : ends + 2 * inner].reshape(2, inner)
    sum_upbias = sums[ends + 2 * inner : used]
    qkv_new = adamw(
        qkv_weight, sum_qkv.reshape(share, 3, inner), qkv_first, qkv_second, 0.1, 0.1
    )
    proj_new = adamw(proj_weight, sum_proj.T, proj_first, proj_second, 1.0, 0.1)
    up_new = adamw(up_weight, sum_up, up_first, up_second, 0.1, 0.1)
    down_new = adamw(down_weight, sum_down.T, down_first, down_second, 0.05, 0.1)
    qbias_new = adamw(qkv_bias, sum_qbias, qbias_first, qbias_second, 1.0, 0.0)
    ubias_new = adamw(up_bias, sum_upbias, ubias_first, ubias_second, 1.0, 0.0)
    vector_new = adamw(layer_vectors, sum_vectors, vector_first, vector_second, 1.0, 0.0)
    return (
        block_output.reshape(seqs, rows, width),
        input_grad.reshape(seqs, rows, width),
        *qkv_new,
        *proj_new,
        *up_new,
        *down_new,
        *qbias_new,
        *ubias_new,
        *vector_new,
    )


def solution(mesh):
    groups = mesh.shape["ctx"]
    tiled = groups % 4 == 0 and WIDTH % (groups * 16) == 0
    return jax.shard_map(
        ring_local if tiled else local,
        mesh=mesh,
        in_specs=(
            P(None, "ctx", None),
            P(None, "ctx", None),
            P(),
            P("ctx", None, "tp"),
            P("tp", "ctx"),
            P("ctx", "tp"),
            P("tp", "ctx"),
            P(None, "tp"),
            P("tp"),
            P(None, "ctx"),
            P("ctx", None, "tp"),
            P("ctx", None, "tp"),
            P("tp", "ctx"),
            P("tp", "ctx"),
            P("ctx", "tp"),
            P("ctx", "tp"),
            P("tp", "ctx"),
            P("tp", "ctx"),
            P(None, "tp"),
            P(None, "tp"),
            P("tp"),
            P("tp"),
            P(None, "ctx"),
            P(None, "ctx"),
        ),
        out_specs=(
            P(None, "ctx", None),
            P(None, "ctx", None),
            P("ctx", None, "tp"),
            P("ctx", None, "tp"),
            P("ctx", None, "tp"),
            P("tp", "ctx"),
            P("tp", "ctx"),
            P("tp", "ctx"),
            P("ctx", "tp"),
            P("ctx", "tp"),
            P("ctx", "tp"),
            P("tp", "ctx"),
            P("tp", "ctx"),
            P("tp", "ctx"),
            P(None, "tp"),
            P(None, "tp"),
            P(None, "tp"),
            P("tp"),
            P("tp"),
            P("tp"),
            P(None, "ctx"),
            P(None, "ctx"),
            P(None, "ctx"),
        ),
        check_vma=False,
    )
```

```python
from functools import partial
import math

import jax
import jax.numpy as jnp
from jax import lax
from jax.experimental import pallas as pl
from jax.experimental.pallas import tpu as pltpu
from jax.sharding import PartitionSpec as P

HD = 64
STEP = 10
WIDTH = 768
MESH = pl.DeviceIdType.MESH
VMEM_LIMIT = 48 * 1024 * 1024


BETA_ONE = 0.9
BETA_TWO = 0.95
EPSILON = 1e-08


def layer_norm(values, gain, shift):
    center = values - jnp.mean(values, axis=-1, keepdims=True)
    spread = jnp.mean(center * center, axis=-1, keepdims=True)
    return center * lax.rsqrt(spread + 1e-05) * gain + shift


def gelu_tanh(values):
    return (
        0.5
        * values
        * (1.0 + jnp.tanh(0.7978845608028654 * (values + 0.044715 * values * values * values)))
    )


def adamw(weight, grad, first, second, rate, decay):
    first_new = BETA_ONE * first + (1.0 - BETA_ONE) * grad
    second_new = BETA_TWO * second + (1.0 - BETA_TWO) * grad * grad
    first_hat = first_new / (1.0 - BETA_ONE**STEP)
    second_hat = second_new / (1.0 - BETA_TWO**STEP)
    weight_new = weight - rate * (first_hat / (jnp.sqrt(second_hat) + EPSILON) + decay * weight)
    return (weight_new, first_new, second_new)


def block_positions(order, start, count, blk):
    blocks = lax.dynamic_slice_in_dim(order, start // blk, count // blk, 1)
    offsets = jnp.arange(blk, dtype=jnp.int32)
    return (blocks[:, :, None] * blk + offsets[None, None, :]).reshape(order.shape[0], count)


def row_blocks(array, size):
    shape = array.shape
    return jnp.moveaxis(array.reshape((shape[0], shape[1] // size, size) + shape[2:]), 1, 0)


def forward_fold(carry, piece, start, queries, query_pos, order, blk):
    key_rows, value_rows = piece
    seqs, count, width = key_rows.shape
    heads = width // HD
    size = math.gcd(count, 512)
    key_pos = block_positions(order, start, count, blk)

    def step(state, block):
        key_block, value_block, place_block = block
        running_max, running_sum, context_sum = state
        key_heads = key_block.reshape(seqs, size, heads, HD)
        value_heads = value_block.reshape(seqs, size, heads, HD)
        scores = (
            jnp.einsum("sqhd,skhd->shqk", queries, key_heads, preferred_element_type=jnp.float32)
            * 0.125
        )
        allowed = query_pos[:, None, :, None] >= place_block[:, None, None, :]
        scores = jnp.where(allowed, scores, -1000000000.0)
        top_now = jnp.maximum(running_max, jnp.max(scores, axis=-1))
        rescale = jnp.exp(running_max - top_now)
        shares = jnp.exp(scores - top_now[..., None])
        running_sum = running_sum * rescale + jnp.sum(shares, axis=-1)
        context_sum = context_sum * rescale[..., None] + jnp.einsum(
            "shqk,skhd->shqd",
            shares.astype(jnp.bfloat16),
            value_heads,
            preferred_element_type=jnp.float32,
        )
        return ((top_now, running_sum, context_sum), None)

    carry, _ = lax.scan(
        step,
        carry,
        (row_blocks(key_rows, size), row_blocks(value_rows, size), row_blocks(key_pos, size)),
    )
    return carry


def keeping_fold(carry, piece, start, forward_step):
    state, key_store, value_store = carry
    key_rows, value_rows = piece
    key_store = key_rows
    value_store = value_rows
    state = forward_step(state, piece, start)
    return (state, key_store, value_store)


def query_fold(carry, piece, start, queries, grad_heads, log_total, delta, query_pos, order, blk):
    key_rows, value_rows = piece
    seqs, count, width = key_rows.shape
    heads = width // HD
    size = math.gcd(count, 512)
    key_pos = block_positions(order, start, count, blk)

    def step(grad_sum, block):
        key_block, value_block, place_block = block
        key_heads = key_block.reshape(seqs, size, heads, HD)
        value_heads = value_block.reshape(seqs, size, heads, HD)
        scores = (
            jnp.einsum("sqhd,skhd->shqk", queries, key_heads, preferred_element_type=jnp.float32)
            * 0.125
        )
        allowed = query_pos[:, None, :, None] >= place_block[:, None, None, :]
        scores = jnp.where(allowed, scores, -1000000000.0)
        shares = jnp.exp(scores - log_total[..., None])
        grad_share = jnp.einsum(
            "sqhd,skhd->shqk", grad_heads, value_heads, preferred_element_type=jnp.float32
        )
        grad_score = shares * (grad_share - delta[..., None])
        grad_sum = (
            grad_sum
            + jnp.einsum(
                "shqk,skhd->shqd",
                grad_score.astype(jnp.bfloat16),
                key_heads,
                preferred_element_type=jnp.float32,
            )
            * 0.125
        )
        return (grad_sum, None)

    carry, _ = lax.scan(
        step,
        carry,
        (row_blocks(key_rows, size), row_blocks(value_rows, size), row_blocks(key_pos, size)),
    )
    return carry


def key_fold(carry, piece, start, key_heads, value_heads, key_pos, order, blk):
    query_rows, grad_rows, log_rows, delta_rows = piece
    seqs, count, width = query_rows.shape
    heads = width // HD
    size = math.gcd(count, 512)
    query_pos = block_positions(order, start, count, blk)

    def step(state, block):
        grad_keys, grad_values = state
        query_block, grad_block, log_block, delta_block, place_block = block
        query_heads = query_block.reshape(seqs, size, heads, HD)
        grad_heads = grad_block.reshape(seqs, size, heads, HD)
        log_heads = jnp.transpose(log_block, (0, 2, 1))
        delta_heads = jnp.transpose(delta_block, (0, 2, 1))
        scores = (
            jnp.einsum(
                "sihd,sjhd->shij", query_heads, key_heads, preferred_element_type=jnp.float32
            )
            * 0.125
        )
        allowed = place_block[:, None, :, None] >= key_pos[:, None, None, :]
        scores = jnp.where(allowed, scores, -1000000000.0)
        shares = jnp.exp(scores - log_heads[..., None])
        grad_values = grad_values + jnp.einsum(
            "shij,sihd->shjd",
            shares.astype(jnp.bfloat16),
            grad_heads,
            preferred_element_type=jnp.float32,
        )
        grad_share = jnp.einsum(
            "sihd,sjhd->shij", grad_heads, value_heads, preferred_element_type=jnp.float32
        )
        grad_score = shares * (grad_share - delta_heads[..., None])
        grad_keys = (
            grad_keys
            + jnp.einsum(
                "shij,sihd->shjd",
                grad_score.astype(jnp.bfloat16),
                query_heads,
                preferred_element_type=jnp.float32,
            )
            * 0.125
        )
        return ((grad_keys, grad_values), None)

    carry, _ = lax.scan(
        step,
        carry,
        (
            row_blocks(query_rows, size),
            row_blocks(grad_rows, size),
            row_blocks(log_rows, size),
            row_blocks(delta_rows, size),
            row_blocks(query_pos, size),
        ),
    )
    return carry


def local(
    tokens,
    out_grad,
    block_order,
    qkv_weight,
    proj_weight,
    up_weight,
    down_weight,
    qkv_bias,
    up_bias,
    layer_vectors,
    qkv_first,
    qkv_second,
    proj_first,
    proj_second,
    up_first,
    up_second,
    down_first,
    down_second,
    qbias_first,
    qbias_second,
    ubias_first,
    ubias_second,
    vector_first,
    vector_second,
):
    device = lax.axis_index("ctx")
    groups = lax.axis_size("ctx")
    seqs, rows, width = tokens.shape
    blk = rows // 2
    query_pos = block_positions(block_order, device * rows, rows, blk)
    qkv_full, up_full, proj_full, down_full = (
        lax.all_gather(qkv_weight.astype(jnp.bfloat16), "ctx", axis=0, tiled=True),
        lax.all_gather(up_weight.astype(jnp.bfloat16), "ctx", axis=0, tiled=True),
        lax.all_gather(proj_weight.astype(jnp.bfloat16), "ctx", axis=1, tiled=True),
        lax.all_gather(down_weight.astype(jnp.bfloat16), "ctx", axis=1, tiled=True),
    )
    layer_vector_rows = lax.all_gather(layer_vectors, "ctx", axis=1, tiled=True)
    inputs = tokens.astype(jnp.float32)
    first_normalized, norm_one_back = jax.vjp(
        layer_norm, inputs, layer_vector_rows[0], layer_vector_rows[1]
    )
    normed_low = first_normalized.astype(jnp.bfloat16)
    projection_output = jnp.einsum(
        "sqd,dcf->sqcf", normed_low, qkv_full, preferred_element_type=jnp.float32
    )
    queries = (projection_output[:, :, 0] + qkv_bias[0]).astype(jnp.bfloat16)
    keys = projection_output[:, :, 1].astype(jnp.bfloat16)
    values = (projection_output[:, :, 2] + qkv_bias[1]).astype(jnp.bfloat16)
    heads = queries.shape[-1] // HD
    query_heads = queries.reshape(seqs, rows, heads, HD)
    key_heads = keys.reshape(seqs, rows, heads, HD)
    value_heads = values.reshape(seqs, rows, heads, HD)
    start_state = (
        jnp.full((seqs, heads, rows), -1e30, jnp.float32),
        jnp.zeros((seqs, heads, rows), jnp.float32),
        jnp.zeros((seqs, heads, rows, HD), jnp.float32),
    )
    forward_step = partial(
        forward_fold, queries=query_heads, query_pos=query_pos, order=block_order, blk=blk
    )
    empty_store = jnp.zeros((seqs, rows * groups, keys.shape[-1]), jnp.bfloat16)
    folded, key_store, value_store = keeping_fold(
        (start_state, empty_store, empty_store),
        (
            lax.all_gather(keys, "ctx", axis=1, tiled=True),
            lax.all_gather(values, "ctx", axis=1, tiled=True),
        ),
        jnp.int32(0),
        forward_step=forward_step,
    )
    running_max, running_sum, context_sum = folded
    whole_pair = (key_store, value_store)
    log_total = running_max + jnp.log(running_sum)
    context_value = context_sum / running_sum[..., None]
    context_rows = jnp.transpose(context_value, (0, 2, 1, 3)).reshape(seqs, rows, heads * HD)
    context_low = context_rows.astype(jnp.bfloat16)
    attn_part = jnp.einsum(
        "sqf,fd->sqd", context_low, proj_full, preferred_element_type=jnp.float32
    )
    attention_result = lax.psum(attn_part, "tp") + layer_vector_rows[4]
    middle = inputs + attention_result
    second_normalized, norm_two_back = jax.vjp(
        layer_norm, middle, layer_vector_rows[2], layer_vector_rows[3]
    )
    normed_mid = second_normalized.astype(jnp.bfloat16)
    hidden_preactivation = (
        jnp.einsum("sqd,df->sqf", normed_mid, up_full, preferred_element_type=jnp.float32) + up_bias
    )
    hidden_activation, gelu_back = jax.vjp(gelu_tanh, hidden_preactivation)
    hidden_low = hidden_activation.astype(jnp.bfloat16)
    mlp_part = jnp.einsum("sqf,fd->sqd", hidden_low, down_full, preferred_element_type=jnp.float32)
    mlp_total = lax.psum(mlp_part, "tp") + layer_vector_rows[5]
    block_output = (middle + mlp_total).astype(jnp.bfloat16)
    grad_out = out_grad.astype(jnp.float32)
    grad_down = jnp.einsum("sqf,sqd->fd", hidden_low, out_grad, preferred_element_type=jnp.float32)
    grad_hidden = jnp.einsum("sqd,fd->sqf", out_grad, down_full, preferred_element_type=jnp.float32)
    grad_pre = gelu_back(grad_hidden)[0].astype(jnp.bfloat16)
    grad_up = jnp.einsum("sqd,sqf->df", normed_mid, grad_pre, preferred_element_type=jnp.float32)
    grad_upbias = jnp.sum(grad_pre.astype(jnp.float32), axis=(0, 1))
    mid_part = jnp.einsum("sqf,df->sqd", grad_pre, up_full, preferred_element_type=jnp.float32)
    grad_normed_two = lax.psum(mid_part, "tp")
    grad_mid_norm, grad_gain_two, grad_shift_two = norm_two_back(grad_normed_two)
    grad_middle = grad_out + grad_mid_norm
    grad_attn = grad_middle.astype(jnp.bfloat16)
    grad_proj = jnp.einsum(
        "sqf,sqd->fd", context_low, grad_attn, preferred_element_type=jnp.float32
    )
    grad_context = jnp.einsum(
        "sqd,fd->sqf", grad_attn, proj_full, preferred_element_type=jnp.float32
    ).astype(jnp.bfloat16)
    grad_heads = grad_context.reshape(seqs, rows, heads, HD)
    row_delta = jnp.sum(
        grad_heads.astype(jnp.float32) * context_rows.reshape(seqs, rows, heads, HD), axis=-1
    )
    delta_heads = jnp.transpose(row_delta, (0, 2, 1))
    log_rows = jnp.transpose(log_total, (0, 2, 1))
    zero_heads = jnp.zeros((seqs, heads, rows, HD), jnp.float32)
    query_step = partial(
        query_fold,
        queries=query_heads,
        grad_heads=grad_heads,
        log_total=log_total,
        delta=delta_heads,
        query_pos=query_pos,
        order=block_order,
        blk=blk,
    )
    grad_q_sum = query_step(zero_heads, whole_pair, 0)
    key_step = partial(
        key_fold,
        key_heads=key_heads,
        value_heads=value_heads,
        key_pos=query_pos,
        order=block_order,
        blk=blk,
    )
    grad_k_sum, grad_v_sum = key_step(
        (zero_heads, zero_heads),
        (
            lax.all_gather(queries.astype(jnp.float32), "ctx", axis=1, tiled=True).astype(
                jnp.bfloat16
            ),
            lax.all_gather(grad_context.astype(jnp.float32), "ctx", axis=1, tiled=True).astype(
                jnp.bfloat16
            ),
            lax.all_gather(log_rows, "ctx", axis=1, tiled=True),
            lax.all_gather(row_delta, "ctx", axis=1, tiled=True),
        ),
        jnp.int32(0),
    )

    def head_rows(array):
        return (
            jnp.transpose(array, (0, 2, 1, 3)).reshape(seqs, rows, heads * HD).astype(jnp.bfloat16)
        )

    grad_qkv_low = jnp.stack(
        [head_rows(grad_q_sum), head_rows(grad_k_sum), head_rows(grad_v_sum)], axis=2
    )
    grad_qkv = jnp.einsum(
        "sqd,sqcf->dcf", normed_low, grad_qkv_low, preferred_element_type=jnp.float32
    )
    grad_qbias = jnp.sum(grad_qkv_low[:, :, 0::2].astype(jnp.float32), axis=(0, 1))
    first_part = jnp.einsum(
        "sqcf,dcf->sqd", grad_qkv_low, qkv_full, preferred_element_type=jnp.float32
    )
    grad_normed_one = lax.psum(first_part, "tp")
    grad_in_norm, grad_gain_one, grad_shift_one = norm_one_back(grad_normed_one)
    input_grad = grad_middle + grad_in_norm
    grad_vectors = jnp.stack(
        [
            grad_gain_one,
            grad_shift_one,
            grad_gain_two,
            grad_shift_two,
            jnp.sum(grad_attn.astype(jnp.float32), axis=(0, 1)),
            jnp.sum(grad_out, axis=(0, 1)),
        ]
    )
    sum_qkv, sum_up, sum_proj, sum_down, sum_vectors = (
        lax.psum_scatter(grad_qkv, "ctx", scatter_dimension=0, tiled=True),
        lax.psum_scatter(grad_up, "ctx", scatter_dimension=0, tiled=True),
        lax.psum_scatter(grad_proj, "ctx", scatter_dimension=1, tiled=True),
        lax.psum_scatter(grad_down, "ctx", scatter_dimension=1, tiled=True),
        lax.psum_scatter(grad_vectors, "ctx", scatter_dimension=1, tiled=True),
    )
    sum_qbias, sum_upbias = lax.psum((grad_qbias, grad_upbias), "ctx")
    qkv_new = adamw(qkv_weight, sum_qkv, qkv_first, qkv_second, 0.1, 0.1)
    proj_new = adamw(proj_weight, sum_proj, proj_first, proj_second, 1.0, 0.1)
    up_new = adamw(up_weight, sum_up, up_first, up_second, 0.1, 0.1)
    down_new = adamw(down_weight, sum_down, down_first, down_second, 0.05, 0.1)
    qbias_new = adamw(qkv_bias, sum_qbias, qbias_first, qbias_second, 1.0, 0.0)
    ubias_new = adamw(up_bias, sum_upbias, ubias_first, ubias_second, 1.0, 0.0)
    vector_new = adamw(layer_vectors, sum_vectors, vector_first, vector_second, 1.0, 0.0)
    return (
        block_output,
        input_grad,
        qkv_new[0],
        qkv_new[1],
        qkv_new[2],
        proj_new[0],
        proj_new[1],
        proj_new[2],
        up_new[0],
        up_new[1],
        up_new[2],
        down_new[0],
        down_new[1],
        down_new[2],
        qbias_new[0],
        qbias_new[1],
        qbias_new[2],
        ubias_new[0],
        ubias_new[1],
        ubias_new[2],
        vector_new[0],
        vector_new[1],
        vector_new[2],
    )


def chip_at(place, chips):
    half = chips // 2
    back = place // half
    return (1 - back) * 2 * place + back * (2 * (chips - 1 - place) + 1)


class Ring:
    def __init__(self, chips):
        me = lax.axis_index("ctx")
        self.chips, self.me = chips, me
        self.core = me % 2
        chip = me // 2
        along, across = chip // 2, chip % 2
        self.place = along + across * (chips - 1 - 2 * along)
        self.right, self.left = self.slot(1), self.slot(-1)
        self.mate = chip * 2 + 1 - self.core

    def slot(self, ahead, other=False):
        place = (self.place + ahead + 2 * self.chips) % self.chips
        core = 1 - self.core if other else self.core
        return chip_at(place, self.chips) * 2 + core

    def greet(self, count=3):
        barrier = pltpu.get_barrier_semaphore()
        for device in (self.left, self.right, self.mate):
            pl.semaphore_signal(barrier, inc=1, device_id={"ctx": device}, device_id_type=MESH)
        pl.semaphore_wait(barrier, count)


def remote(src, dst, send, recv, device):
    return pltpu.make_async_remote_copy(
        src_ref=src,
        dst_ref=dst,
        send_sem=send,
        recv_sem=recv,
        device_id={"ctx": device},
        device_id_type=MESH,
    )


class Gather:
    def __init__(self, ring, ins, outs, sems):
        self.ring, self.ins, self.outs = ring, ins, outs
        self.ring_send, self.ring_recv, self.mate_send, self.mate_recv, self.own = sems
        self.far_right = ring.chips // 2
        self.far_left = ring.chips - 1 - self.far_right
        self.sent = []

    def hop(self, at, src, slot, step, sign):
        columns, last = slice(None), step == self.far_right - 1
        if last:
            width = src.shape[-1]
            cut = (width + 128) // 256 * 128
            columns = slice(0, cut) if sign > 0 else slice(cut, width)
        index = step if sign > 0 else self.far_right + step
        return remote(
            src.at[:, columns] if last else src,
            self.outs[at].at[slot, :, columns] if last else self.outs[at].at[slot],
            self.ring_send.at[at, index], self.ring_recv.at[at, index],
            self.ring.right if sign > 0 else self.ring.left,
        )

    def pass_on(self, at, src, slot, index):
        copy = remote(
            src, self.outs[at].at[slot], self.mate_send.at[at, index],
            self.mate_recv.at[at, index], self.ring.mate,
        )
        return copy

    def go(self, copy):
        copy.start()
        self.sent.append(copy)

    def start(self):
        ring = self.ring
        for at, block in enumerate(self.ins):
            self.go(self.hop(at, block, ring.me, 0, 1))
            self.go(self.hop(at, block, ring.me, 0, -1))
            self.go(self.pass_on(at, block, ring.me, 0))
            pltpu.make_async_copy(block, self.outs[at].at[ring.me], self.own.at[at]).start()

    def step(self, step):
        ring = self.ring
        last = step == self.far_right - 1
        for at in range(len(self.ins)):
            for sign in (1, -1):
                slot = ring.slot(-sign * (step + 1))
                block = self.outs[at].at[slot]
                self.hop(at, block, slot, step, sign).wait_recv()
                if not last:
                    self.go(self.hop(at, block, slot, step + 1, sign))
                if not last or sign < 0:
                    index = 1 + step if last or sign > 0 else 1 + self.far_right + step
                    self.go(self.pass_on(at, block, slot, index))

    def finish(self):
        ring = self.ring
        for at in range(len(self.ins)):
            order = [0] + [-(s + 1) for s in range(self.far_right)]
            order += [s + 1 for s in range(self.far_left)]
            for index, ahead in enumerate(order):
                slot = ring.slot(ahead, other=True)
                self.pass_on(at, self.outs[at].at[slot], slot, index).wait_recv()
            pltpu.make_async_copy(
                self.ins[at], self.outs[at].at[ring.me], self.own.at[at]
            ).wait()
        for copy in self.sent:
            copy.wait_send()


def gather_sems(count, chips):
    return [pltpu.SemaphoreType.DMA((count, chips))] * 4 + [pltpu.SemaphoreType.DMA((count,))]


class Scatter:
    def __init__(self, ring, pieces, grads, mates, lands, outs, sems):
        self.ring, self.pieces = ring, pieces
        self.grads, self.mates, self.lands, self.outs = grads, mates, lands, outs
        self.mate_send, self.mate_recv, self.ring_send, self.ring_recv = sems
        self.order = []
        for far in range(1, ring.chips // 2):
            self.order += [-far, far]
        self.order += [ring.chips // 2, 0]
        self.arrived = set()
        self.sent = []

    def to_mate(self, index, at):
        ring = self.ring
        return remote(
            self.grads[at].at[ring.slot(self.order[index], other=True)],
            self.mates[at].at[index],
            self.mate_send.at[at, index], self.mate_recv.at[at, index], ring.mate,
        )

    def start(self):
        for index in range(self.ring.chips):
            for at in range(len(self.grads)):
                copy = self.to_mate(index, at)
                copy.start()
                self.sent.append(copy)

    def own_part(self, ahead, at, columns):
        half = self.ring.chips // 2 - 1
        ahead = (ahead + half) % self.ring.chips - half
        index = self.order.index(ahead)
        if (index, at) not in self.arrived:
            self.arrived.add((index, at))
            self.to_mate(index, at).wait_recv()
        mine = self.grads[at][self.ring.slot(ahead), :, columns].astype(jnp.float32)
        return mine + self.mates[at][index, :, columns].astype(jnp.float32)

    def hop(self, which, step, src):
        device = self.ring.right if self.pieces[which][3] > 0 else self.ring.left
        return remote(
            src, self.lands[which].at[step], self.ring_send.at[which, step],
            self.ring_recv.at[which, step], device,
        )

    def step(self, step):
        chips = self.ring.chips
        for which, (at, first, count, sign) in enumerate(self.pieces):
            columns = slice(first, first + count)
            land = self.lands[which]
            part = self.own_part(-sign * (step + 1), at, columns)
            if step > 0:
                self.hop(which, step - 1, land.at[step - 1]).wait_recv()
                part = part + land[step - 1].astype(jnp.float32)
            if step < chips - 1:
                hold = land.at[chips - 1 + step]
                hold[...] = part.astype(jnp.bfloat16)
                copy = self.hop(which, step, hold)
                copy.start()
                self.sent.append(copy)
            else:
                self.outs[at][:, columns] = part

    def finish(self):
        for copy in self.sent:
            copy.wait_send()


def scatter_scratch(blocks, pieces, chips):
    rows, dma = blocks[0].shape[1], pltpu.SemaphoreType.DMA
    return (
        [pltpu.VMEM((chips, rows, b.shape[2]), jnp.bfloat16) for b in blocks]
        + [pltpu.VMEM((2 * chips - 2, rows, p[2]), jnp.bfloat16) for p in pieces]
        + [dma((len(blocks), chips))] * 2
        + [dma((len(pieces), chips))] * 2
    )


def row_split(array, groups):
    return array.reshape(groups, array.shape[0] // groups, array.shape[1])


def pair_kernel(count, *refs):
    ins, outs = refs[:count], refs[count : 2 * count]
    holds, lands = refs[2 * count : 3 * count], refs[3 * count : 4 * count]
    send, recv = refs[4 * count :]
    other = 1 - lax.axis_index("tp")
    barrier = pltpu.get_barrier_semaphore()
    pl.semaphore_signal(barrier, inc=1, device_id={"tp": other}, device_id_type=MESH)
    for at in range(count):
        holds[at][...] = ins[at][...].astype(jnp.bfloat16)
    pl.semaphore_wait(barrier, 1)
    copies = []
    for at in range(count):
        copy = pltpu.make_async_remote_copy(
            src_ref=holds[at], dst_ref=lands[at], send_sem=send.at[at], recv_sem=recv.at[at],
            device_id={"tp": other}, device_id_type=MESH,
        )
        copy.start()
        copies.append(copy)
    for at in range(count):
        copies[at].wait()
        outs[at][...] = holds[at][...].astype(jnp.float32) + lands[at][...].astype(jnp.float32)


def pair_sum(arrays, collective):
    count = len(arrays)
    vmem = pl.BlockSpec(memory_space=pltpu.VMEM)
    return pl.pallas_call(
        partial(pair_kernel, count),
        out_shape=[jax.ShapeDtypeStruct(a.shape, jnp.float32) for a in arrays],
        in_specs=[vmem] * count,
        out_specs=[vmem] * count,
        scratch_shapes=[pltpu.VMEM(a.shape, jnp.bfloat16) for a in arrays] * 2
        + [pltpu.SemaphoreType.DMA((count,))] * 2,
        compiler_params=pltpu.CompilerParams(
            collective_id=collective, has_side_effects=True, vmem_limit_bytes=VMEM_LIMIT
        ),
    )(*arrays)


NT = (((1,), (1,)), ((), ()))
NN = (((1,), (0,)), ((), ()))


def mul(left, right, dims):
    return lax.dot_general(left, right, dims, preferred_element_type=jnp.float32)


def attend_unit(heads, seq, head, rows, allowed, own, every, context_ref):
    width = heads * HD
    here = slice(seq * rows, (seq + 1) * rows)
    at = slice(head * HD, (head + 1) * HD)
    keys = every[:, here, width + head * HD : width + (head + 1) * HD].reshape(-1, HD)
    values = every[:, here, 2 * width + head * HD : 2 * width + (head + 1) * HD].reshape(-1, HD)
    scores = mul(own(here, at), keys, NT) * 0.125
    scores = jnp.where(allowed, scores, -1000000000.0)
    top = jnp.max(scores, axis=-1, keepdims=True)
    shares = jnp.exp(scores - top)
    total = jnp.sum(shares, axis=-1, keepdims=True)
    mixed = mul(shares.astype(jnp.bfloat16), values, NN)
    context_ref[here, at] = mixed / total
    return top + jnp.log(total)


def front_kernel(chips, heads, *refs):
    ins, (bias, own_pos, all_pos) = refs[0:5], refs[5:8]
    outs, vectors_ref, every, context_ref, log_ref = refs[8:13], *refs[13:17]
    tokens_all, lows, sems = outs[1], refs[17:20], refs[20:]
    width = heads * HD
    groups = 2 * chips
    seqs = own_pos.shape[0]
    rows = tokens_all.shape[1] // seqs
    ring = Ring(chips)
    ring.greet()
    first = Gather(ring, ins[0:2], outs[0:2], sems[0:5])
    second = Gather(ring, lows, outs[2:5], sems[5:10])
    first.start()
    for low, weight in zip(lows, ins[2:5]):
        low[...] = weight[...].astype(jnp.bfloat16)
    for step in range(first.far_right - 1):
        first.step(step)
    second.start()
    first.step(first.far_right - 1)
    first.finish()
    packed = outs[0]
    extra = packed[:, :, 3 * width :].reshape(-1, 128).astype(jnp.float32).T
    vectors = (extra[0:6] + extra[6:12]) + extra[12:18]
    vectors_ref[0:6, :] = vectors
    gain, shift = vectors[0:1], vectors[1:2]

    def project(at, carry):
        values = tokens_all[pl.ds(2 * at, 2)].reshape(-1, tokens_all.shape[2])
        normed = layer_norm(values.astype(jnp.float32), gain, shift).astype(jnp.bfloat16)
        weights = packed[:, :, : 3 * width].reshape(-1, 3 * width)
        result = (mul(normed, weights, NN) + bias[...]).astype(jnp.bfloat16)
        every[pl.ds(2 * at, 2)] = result.reshape(2, -1, 3 * width)
        return carry

    lax.fori_loop(0, groups // 4, project, 0)
    second.step(0)
    lax.fori_loop(groups // 4, groups // 2, project, 0)
    second.step(1)

    def own(here, at):
        return every[ring.me, here, at]

    lanes = lax.broadcasted_iota(jnp.int32, (rows, 128), 1)
    for seq in range(seqs):
        allowed = own_pos[seq] >= all_pos[seq]
        logs = jnp.zeros((rows, 128), jnp.float32)
        for head in range(heads):
            log = attend_unit(heads, seq, head, rows, allowed, own, every, context_ref)
            logs = jnp.where(lanes == head, log, logs)
        log_ref[seq * rows : (seq + 1) * rows, :] = logs
        if seq + 2 < second.far_right:
            second.step(seq + 2)
    for step in range(seqs + 2, second.far_right):
        second.step(step)
    second.finish()


def front(arrays, bias, own_pos, all_pos, heads, groups, collective):
    vmem = pl.BlockSpec(memory_space=pltpu.VMEM)
    hbm = pl.BlockSpec(memory_space=pl.ANY)
    many, width = arrays[1].shape
    chips = groups // 2
    return pl.pallas_call(
        partial(front_kernel, chips, heads),
        out_shape=[jax.ShapeDtypeStruct((groups,) + a.shape, jnp.bfloat16) for a in arrays]
        + [
            jax.ShapeDtypeStruct((8, width), jnp.float32),
            jax.ShapeDtypeStruct((groups, many, 3 * heads * HD), jnp.bfloat16),
            jax.ShapeDtypeStruct((many, heads * HD), jnp.float32),
            jax.ShapeDtypeStruct((many, 128), jnp.float32),
        ],
        in_specs=[vmem] * 8,
        out_specs=[vmem] * 2 + [hbm] * 3 + [vmem] * 4,
        scratch_shapes=[pltpu.VMEM(a.shape, jnp.bfloat16) for a in arrays[2:5]]
        + gather_sems(2, chips)
        + gather_sems(3, chips),
        compiler_params=pltpu.CompilerParams(
            collective_id=collective, has_side_effects=True, vmem_limit_bytes=VMEM_LIMIT
        ),
    )(*arrays, bias, own_pos, all_pos)


def token_sum(array):
    return jnp.sum(array.astype(jnp.float32), axis=0, keepdims=True)


def back_kernel(chips, heads, pieces, lone, *refs):
    own, every, own_pos, all_pos = refs[0:4]
    grad_attn, context, normed_mid, grad_pre, grad_low, hidden = refs[4:10]
    normed, packed, normal, grad_two, normal_two = refs[10:15]
    total, sums, small_out = refs[15], refs[16:20], refs[20]
    out_ref, hold, land, small, gathered = refs[21:26]
    grads, rest = refs[26:30], refs[30:]
    many = len(pieces)
    mates, lands, sems, rest = rest[0:3], rest[3 : 3 + many], rest[3 + many : 7 + many], rest[7 + many :]
    alone = len(lone)
    mate, lone_lands, lone_sems = rest[0:1], rest[1 : 1 + alone], rest[1 + alone : 5 + alone]
    pair_send, pair_recv = rest[5 + alone : 7 + alone]
    gather_one, gather_two = rest[7 + alone : 12 + alone], rest[12 + alone : 17 + alone]
    seqs = own_pos.shape[0]
    rows = own.shape[0] // seqs
    width = heads * HD
    other = 1 - lax.axis_index("tp")
    ring = Ring(chips)
    me = ring.me
    barrier = pltpu.get_barrier_semaphore()
    pl.semaphore_signal(barrier, inc=1, device_id={"tp": other}, device_id_type=MESH)
    ring.greet(4)
    gather = Gather(ring, [own], [gathered], gather_one)
    scatter = Scatter(ring, pieces, grads[0:3], mates, lands, sums[0:3], sems)
    lone_scatter = Scatter(ring, lone, grads[3:4], mate, lone_lands, sums[3:4], lone_sems)

    def product(into, left, right):
        blocks = into.shape[0] // 2
        high = blocks * into.shape[1]
        for half in range(2):
            result = lax.dot_general(
                left[:, half * high : (half + 1) * high], right[...],
                (((0,), (0,)), ((), ())), preferred_element_type=jnp.float32,
            )
            into[half * blocks : (half + 1) * blocks] = result.astype(jnp.bfloat16).reshape(
                (blocks,) + into.shape[1:]
            )

    gather.start()
    product(grads[2], grad_low, hidden)
    gather.step(0)
    product(grads[1], normed_mid, grad_pre)
    gather.step(1)
    product(grads[0], grad_attn, context)
    scatter.start()
    for step in range(2, gather.far_right - 1):
        gather.step(step)
    scatter.step(0)
    gather.step(gather.far_right - 1)
    gather.finish()
    done = 1
    for seq in range(seqs):
        here = slice(seq * rows, (seq + 1) * rows)
        allowed = own_pos[seq] >= all_pos[seq]
        allowed_back = own_pos[seq] <= all_pos[seq]
        stats = gathered[:, here, width:].reshape(-1, 128).astype(jnp.float32).T
        turned = (stats[0:16] + stats[16:32]) + stats[32:48]
        parts = own[here, width:].astype(jnp.float32)
        stat = (parts[:, 0:16] + parts[:, 16:32]) + parts[:, 32:48]
        for head in range(heads):
            at = slice(head * HD, (head + 1) * HD)
            past = slice(width + head * HD, width + (head + 1) * HD)
            last = slice(2 * width + head * HD, 2 * width + (head + 1) * HD)
            queries = every[:, here, at].reshape(-1, HD)
            keys = every[:, here, past].reshape(-1, HD)
            values = every[:, here, last].reshape(-1, HD)
            grad_all = gathered[:, here, at].reshape(-1, HD)
            query, key, value = every[me, here, at], every[me, here, past], every[me, here, last]
            scores = jnp.where(allowed, mul(query, keys, NT) * 0.125, -1000000000.0)
            shares = jnp.exp(scores - stat[:, head : head + 1])
            grad_share = mul(own[here, at], values, NT)
            delta = stat[:, heads + head : heads + head + 1]
            grad_score = (shares * (grad_share - delta)).astype(jnp.bfloat16)
            out_ref[here, at] = (mul(grad_score, keys, NN) * 0.125).astype(jnp.bfloat16)
            scores = jnp.where(allowed_back, mul(key, queries, NT) * 0.125, -1000000000.0)
            shares = jnp.exp(scores - turned[head : head + 1])
            grad_value = mul(shares.astype(jnp.bfloat16), grad_all, NN)
            grad_share = mul(value, grad_all, NT)
            grad_score = shares * (grad_share - turned[heads + head : heads + head + 1])
            grad_key = mul(grad_score.astype(jnp.bfloat16), queries, NN) * 0.125
            out_ref[here, past] = grad_key.astype(jnp.bfloat16)
            out_ref[here, last] = grad_value.astype(jnp.bfloat16)
            if head % 3 == 2 and done < chips - 1:
                scatter.step(done)
                done += 1
    weights = packed[:, :, : 3 * width].reshape(-1, 3 * width)
    hold[...] = mul(out_ref[...], weights, NT).astype(jnp.bfloat16)
    pair = pltpu.make_async_remote_copy(
        src_ref=hold, dst_ref=land, send_sem=pair_send.at[0], recv_sem=pair_recv.at[0],
        device_id={"tp": other}, device_id_type=MESH,
    )
    pair.start()
    product(grads[3], normed, out_ref)
    lone_scatter.start()
    if done < chips:
        scatter.step(done)
    lone_scatter.step(0)
    small[...] = jnp.zeros_like(small)
    small[2:3, :] = jnp.sum(grad_two[...] * normal_two[...], axis=0, keepdims=True)
    small[3:4, :] = token_sum(grad_two[...])
    small[4:5, :] = token_sum(grad_attn[...])
    small[5:6, :] = token_sum(grad_low[...])
    small[6:7, 0:width] = token_sum(out_ref[:, 0:width])
    small[7:8, 0:width] = token_sum(out_ref[:, 2 * width : 3 * width])
    span = small.shape[1]
    for at in range(grad_pre.shape[1] // span):
        small[8 + at : 9 + at, :] = token_sum(grad_pre[:, at * span : (at + 1) * span])
    pair.wait()
    summed = hold[...].astype(jnp.float32) + land[...].astype(jnp.float32)
    total[...] = summed
    small[0:1, :] = jnp.sum(summed * normal[...], axis=0, keepdims=True)
    small[1:2, :] = token_sum(summed)
    last = Gather(ring, [small], [small_out], gather_two)
    last.start()
    for step in range(1, chips):
        if done + step < chips:
            scatter.step(done + step)
        lone_scatter.step(step)
        if step - 1 < last.far_right:
            last.step(step - 1)
    for step in range(chips - 1, last.far_right):
        last.step(step)
    last.finish()
    scatter.finish()
    lone_scatter.finish()


def back(arrays, widths, heads, groups, collective):
    vmem = pl.BlockSpec(memory_space=pltpu.VMEM)
    dma = pltpu.SemaphoreType.DMA
    chips = groups // 2
    own = arrays[0]
    many, width = arrays[4].shape
    blocks = [jax.ShapeDtypeStruct((groups, width // groups, w), jnp.bfloat16) for w in widths]
    proj, up, down, qkv = widths
    cut = proj * 2 // 3 // 128 * 128
    pieces = ((1, 0, up, 1), (2, 0, down, -1), (0, 0, cut, 1), (0, cut, proj - cut, -1))
    right = qkv // 256 * 128
    lone = ((0, 0, right, 1), (0, right, qkv - right, -1))
    small = (8 + -(-up // width) + 7) // 8 * 8, width
    return pl.pallas_call(
        partial(back_kernel, chips, heads, pieces, lone),
        out_shape=[jax.ShapeDtypeStruct((many, width), jnp.float32)]
        + [jax.ShapeDtypeStruct(b.shape[1:], jnp.float32) for b in blocks]
        + [jax.ShapeDtypeStruct((groups,) + small, jnp.float32)],
        in_specs=[vmem] * 15,
        out_specs=[vmem] * 6,
        scratch_shapes=[
            pltpu.VMEM((many, qkv), jnp.bfloat16),
            pltpu.VMEM((many, width), jnp.bfloat16),
            pltpu.VMEM((many, width), jnp.bfloat16),
            pltpu.VMEM(small, jnp.float32),
            pltpu.VMEM((groups,) + own.shape, own.dtype),
        ]
        + [pltpu.VMEM(b.shape, b.dtype) for b in blocks]
        + scatter_scratch(blocks[0:3], pieces, chips)
        + scatter_scratch(blocks[3:4], lone, chips)
        + [dma((1,)), dma((1,))]
        + gather_sems(1, chips)
        + gather_sems(1, chips),
        compiler_params=pltpu.CompilerParams(
            collective_id=collective, has_side_effects=True, vmem_limit_bytes=VMEM_LIMIT
        ),
    )(*arrays)


def standard(values):
    center = values - jnp.mean(values, axis=-1, keepdims=True)
    spread = jnp.mean(center * center, axis=-1, keepdims=True)
    return center * lax.rsqrt(spread + 1e-05)


def three_parts(array):
    high = lax.reduce_precision(array, 8, 7)
    rest = array - high
    middle = lax.reduce_precision(rest, 8, 7)
    return [part.astype(jnp.bfloat16) for part in (high, middle, rest - middle)]


def ring_local(
    tokens,
    out_grad,
    block_order,
    qkv_weight,
    proj_weight,
    up_weight,
    down_weight,
    qkv_bias,
    up_bias,
    layer_vectors,
    qkv_first,
    qkv_second,
    proj_first,
    proj_second,
    up_first,
    up_second,
    down_first,
    down_second,
    qbias_first,
    qbias_second,
    ubias_first,
    ubias_second,
    vector_first,
    vector_second,
):
    device = lax.axis_index("ctx")
    groups = lax.axis_size("ctx")
    seqs, rows, width = tokens.shape
    blk = rows // 2
    share = qkv_weight.shape[0]
    inner = qkv_weight.shape[2]
    heads = inner // HD
    many = seqs * rows
    own_pos = block_positions(block_order, device * rows, rows, blk)[:, :, None]
    all_pos = block_positions(block_order, 0, rows * groups, blk)[:, None, :]
    low = jnp.bfloat16
    vector_parts = jnp.concatenate(three_parts(layer_vectors.T), axis=1)
    packed = jnp.concatenate(
        [
            qkv_weight.astype(low).reshape(share, 3 * inner),
            jnp.pad(vector_parts, ((0, 0), (0, 128 - vector_parts.shape[1]))),
        ],
        axis=1,
    )
    bias = jnp.concatenate([qkv_bias[0], jnp.zeros_like(qkv_bias[0]), qkv_bias[1]])[None]
    grad_low = out_grad.reshape(many, width)
    packed_full, _, proj_full, up_full, down_full, vectors, every, context, logs = front(
        [
            packed,
            tokens.reshape(many, width),
            proj_weight.T,
            up_weight,
            down_weight.T,
        ],
        bias,
        own_pos,
        all_pos,
        heads,
        groups,
        1,
    )
    proj_full = proj_full.reshape(width, -1)
    up_full = up_full.reshape(width, -1)
    down_full = down_full.reshape(width, -1)
    inputs = tokens.reshape(many, width).astype(jnp.float32)
    first_normalized, norm_one_back = jax.vjp(layer_norm, inputs, vectors[0], vectors[1])
    normed_low = first_normalized.astype(low)
    normal = standard(inputs)
    context_low = context.astype(low)
    (attn,) = pair_sum([mul(context_low, proj_full, NT)], 3)
    middle = inputs + (attn + vectors[4])
    second_normalized, norm_two_back = jax.vjp(layer_norm, middle, vectors[2], vectors[3])
    normed_mid = second_normalized.astype(low)
    normal_two = standard(middle)
    hidden_preactivation = mul(normed_mid, up_full, NN) + up_bias
    hidden_activation, gelu_back = jax.vjp(gelu_tanh, hidden_preactivation)
    hidden_low = hidden_activation.astype(low)
    grad_hidden = mul(grad_low, down_full, NN)
    grad_pre = gelu_back(grad_hidden)[0].astype(low)
    mlp, grad_normed_two = pair_sum(
        [mul(hidden_low, down_full, NT), mul(grad_pre, up_full, NT)], 4
    )
    block_output = (middle + (mlp + vectors[5])).astype(low)
    grad_out = grad_low.astype(jnp.float32)
    grad_mid_norm = norm_two_back(grad_normed_two)[0]
    grad_middle = grad_out + grad_mid_norm
    grad_attn = grad_middle.astype(low)
    grad_context = mul(grad_attn, proj_full, NN).astype(low)
    lanes = jnp.arange(128)[None, :]
    choose = (lanes == heads + jnp.arange(inner)[:, None] // HD).astype(jnp.float32)
    delta = jnp.dot(
        grad_context.astype(jnp.float32) * context, choose, precision=lax.Precision.HIGHEST
    )
    stats = three_parts((logs + delta)[:, :16])
    own = jnp.concatenate([grad_context] + stats + [jnp.zeros((many, 80), low)], axis=1)

    grad_normed_one, sum_proj, sum_up, sum_down, sum_qkv, all_small = back(
        [
            own, every, own_pos, all_pos,
            grad_attn, context_low, normed_mid, grad_pre, grad_low, hidden_low,
            normed_low, packed_full, normal, grad_normed_two, normal_two,
        ],
        (inner, up_full.shape[1], down_full.shape[1], 3 * inner),
        heads,
        groups,
        5,
    )
    grad_in_norm = norm_one_back(grad_normed_one)[0]
    input_grad = grad_middle + grad_in_norm
    sums = jnp.sum(all_small, axis=0)
    sum_vectors = lax.dynamic_slice_in_dim(sums[0:6], device * share, share, 1)
    sum_qbias = sums[6:8, :inner]
    sum_upbias = sums[8:].reshape(-1)[: up_bias.shape[0]]
    qkv_new = adamw(
        qkv_weight, sum_qkv.reshape(share, 3, inner), qkv_first, qkv_second, 0.1, 0.1
    )
    proj_new = adamw(proj_weight, sum_proj.T, proj_first, proj_second, 1.0, 0.1)
    up_new = adamw(up_weight, sum_up, up_first, up_second, 0.1, 0.1)
    down_new = adamw(down_weight, sum_down.T, down_first, down_second, 0.05, 0.1)
    qbias_new = adamw(qkv_bias, sum_qbias, qbias_first, qbias_second, 1.0, 0.0)
    ubias_new = adamw(up_bias, sum_upbias, ubias_first, ubias_second, 1.0, 0.0)
    vector_new = adamw(layer_vectors, sum_vectors, vector_first, vector_second, 1.0, 0.0)
    return (
        block_output.reshape(seqs, rows, width),
        input_grad.reshape(seqs, rows, width),
        *qkv_new,
        *proj_new,
        *up_new,
        *down_new,
        *qbias_new,
        *ubias_new,
        *vector_new,
    )


def solution(mesh):
    groups = mesh.shape["ctx"]
    tiled = groups >= 16 and groups % 4 == 0 and WIDTH % (groups * 16) == 0
    return jax.shard_map(
        ring_local if tiled else local,
        mesh=mesh,
        in_specs=(
            P(None, "ctx", None),
            P(None, "ctx", None),
            P(),
            P("ctx", None, "tp"),
            P("tp", "ctx"),
            P("ctx", "tp"),
            P("tp", "ctx"),
            P(None, "tp"),
            P("tp"),
            P(None, "ctx"),
            P("ctx", None, "tp"),
            P("ctx", None, "tp"),
            P("tp", "ctx"),
            P("tp", "ctx"),
            P("ctx", "tp"),
            P("ctx", "tp"),
            P("tp", "ctx"),
            P("tp", "ctx"),
            P(None, "tp"),
            P(None, "tp"),
            P("tp"),
            P("tp"),
            P(None, "ctx"),
            P(None, "ctx"),
        ),
        out_specs=(
            P(None, "ctx", None),
            P(None, "ctx", None),
            P("ctx", None, "tp"),
            P("ctx", None, "tp"),
            P("ctx", None, "tp"),
            P("tp", "ctx"),
            P("tp", "ctx"),
            P("tp", "ctx"),
            P("ctx", "tp"),
            P("ctx", "tp"),
            P("ctx", "tp"),
            P("tp", "ctx"),
            P("tp", "ctx"),
            P("tp", "ctx"),
            P(None, "tp"),
            P(None, "tp"),
            P(None, "tp"),
            P("tp"),
            P("tp"),
            P("tp"),
            P(None, "ctx"),
            P(None, "ctx"),
            P(None, "ctx"),
        ),
        check_vma=False,
    )
```

```python
from functools import partial
import math

import jax
import jax.numpy as jnp
from jax import lax
from jax.experimental import pallas as pl
from jax.experimental.pallas import tpu as pltpu
from jax.sharding import PartitionSpec as P

HD = 64
STEP = 10
WIDTH = 768
MESH = pl.DeviceIdType.MESH
VMEM_LIMIT = 48 * 1024 * 1024


BETA_ONE = 0.9
BETA_TWO = 0.95
EPSILON = 1e-08


def layer_norm(values, gain, shift):
    center = values - jnp.mean(values, axis=-1, keepdims=True)
    spread = jnp.mean(center * center, axis=-1, keepdims=True)
    return center * lax.rsqrt(spread + 1e-05) * gain + shift


def gelu_tanh(values):
    return (
        0.5
        * values
        * (1.0 + jnp.tanh(0.7978845608028654 * (values + 0.044715 * values * values * values)))
    )


def adamw(weight, grad, first, second, rate, decay):
    first_new = BETA_ONE * first + (1.0 - BETA_ONE) * grad
    second_new = BETA_TWO * second + (1.0 - BETA_TWO) * grad * grad
    first_hat = first_new / (1.0 - BETA_ONE**STEP)
    second_hat = second_new / (1.0 - BETA_TWO**STEP)
    weight_new = weight - rate * (first_hat / (jnp.sqrt(second_hat) + EPSILON) + decay * weight)
    return (weight_new, first_new, second_new)


def block_positions(order, start, count, blk):
    blocks = lax.dynamic_slice_in_dim(order, start // blk, count // blk, 1)
    offsets = jnp.arange(blk, dtype=jnp.int32)
    return (blocks[:, :, None] * blk + offsets[None, None, :]).reshape(order.shape[0], count)


def row_blocks(array, size):
    shape = array.shape
    return jnp.moveaxis(array.reshape((shape[0], shape[1] // size, size) + shape[2:]), 1, 0)


def forward_fold(carry, piece, start, queries, query_pos, order, blk):
    key_rows, value_rows = piece
    seqs, count, width = key_rows.shape
    heads = width // HD
    size = math.gcd(count, 512)
    key_pos = block_positions(order, start, count, blk)

    def step(state, block):
        key_block, value_block, place_block = block
        running_max, running_sum, context_sum = state
        key_heads = key_block.reshape(seqs, size, heads, HD)
        value_heads = value_block.reshape(seqs, size, heads, HD)
        scores = (
            jnp.einsum("sqhd,skhd->shqk", queries, key_heads, preferred_element_type=jnp.float32)
            * 0.125
        )
        allowed = query_pos[:, None, :, None] >= place_block[:, None, None, :]
        scores = jnp.where(allowed, scores, -1000000000.0)
        top_now = jnp.maximum(running_max, jnp.max(scores, axis=-1))
        rescale = jnp.exp(running_max - top_now)
        shares = jnp.exp(scores - top_now[..., None])
        running_sum = running_sum * rescale + jnp.sum(shares, axis=-1)
        context_sum = context_sum * rescale[..., None] + jnp.einsum(
            "shqk,skhd->shqd",
            shares.astype(jnp.bfloat16),
            value_heads,
            preferred_element_type=jnp.float32,
        )
        return ((top_now, running_sum, context_sum), None)

    carry, _ = lax.scan(
        step,
        carry,
        (row_blocks(key_rows, size), row_blocks(value_rows, size), row_blocks(key_pos, size)),
    )
    return carry


def keeping_fold(carry, piece, start, forward_step):
    state, key_store, value_store = carry
    key_rows, value_rows = piece
    key_store = key_rows
    value_store = value_rows
    state = forward_step(state, piece, start)
    return (state, key_store, value_store)


def query_fold(carry, piece, start, queries, grad_heads, log_total, delta, query_pos, order, blk):
    key_rows, value_rows = piece
    seqs, count, width = key_rows.shape
    heads = width // HD
    size = math.gcd(count, 512)
    key_pos = block_positions(order, start, count, blk)

    def step(grad_sum, block):
        key_block, value_block, place_block = block
        key_heads = key_block.reshape(seqs, size, heads, HD)
        value_heads = value_block.reshape(seqs, size, heads, HD)
        scores = (
            jnp.einsum("sqhd,skhd->shqk", queries, key_heads, preferred_element_type=jnp.float32)
            * 0.125
        )
        allowed = query_pos[:, None, :, None] >= place_block[:, None, None, :]
        scores = jnp.where(allowed, scores, -1000000000.0)
        shares = jnp.exp(scores - log_total[..., None])
        grad_share = jnp.einsum(
            "sqhd,skhd->shqk", grad_heads, value_heads, preferred_element_type=jnp.float32
        )
        grad_score = shares * (grad_share - delta[..., None])
        grad_sum = (
            grad_sum
            + jnp.einsum(
                "shqk,skhd->shqd",
                grad_score.astype(jnp.bfloat16),
                key_heads,
                preferred_element_type=jnp.float32,
            )
            * 0.125
        )
        return (grad_sum, None)

    carry, _ = lax.scan(
        step,
        carry,
        (row_blocks(key_rows, size), row_blocks(value_rows, size), row_blocks(key_pos, size)),
    )
    return carry


def key_fold(carry, piece, start, key_heads, value_heads, key_pos, order, blk):
    query_rows, grad_rows, log_rows, delta_rows = piece
    seqs, count, width = query_rows.shape
    heads = width // HD
    size = math.gcd(count, 512)
    query_pos = block_positions(order, start, count, blk)

    def step(state, block):
        grad_keys, grad_values = state
        query_block, grad_block, log_block, delta_block, place_block = block
        query_heads = query_block.reshape(seqs, size, heads, HD)
        grad_heads = grad_block.reshape(seqs, size, heads, HD)
        log_heads = jnp.transpose(log_block, (0, 2, 1))
        delta_heads = jnp.transpose(delta_block, (0, 2, 1))
        scores = (
            jnp.einsum(
                "sihd,sjhd->shij", query_heads, key_heads, preferred_element_type=jnp.float32
            )
            * 0.125
        )
        allowed = place_block[:, None, :, None] >= key_pos[:, None, None, :]
        scores = jnp.where(allowed, scores, -1000000000.0)
        shares = jnp.exp(scores - log_heads[..., None])
        grad_values = grad_values + jnp.einsum(
            "shij,sihd->shjd",
            shares.astype(jnp.bfloat16),
            grad_heads,
            preferred_element_type=jnp.float32,
        )
        grad_share = jnp.einsum(
            "sihd,sjhd->shij", grad_heads, value_heads, preferred_element_type=jnp.float32
        )
        grad_score = shares * (grad_share - delta_heads[..., None])
        grad_keys = (
            grad_keys
            + jnp.einsum(
                "shij,sihd->shjd",
                grad_score.astype(jnp.bfloat16),
                query_heads,
                preferred_element_type=jnp.float32,
            )
            * 0.125
        )
        return ((grad_keys, grad_values), None)

    carry, _ = lax.scan(
        step,
        carry,
        (
            row_blocks(query_rows, size),
            row_blocks(grad_rows, size),
            row_blocks(log_rows, size),
            row_blocks(delta_rows, size),
            row_blocks(query_pos, size),
        ),
    )
    return carry


def local(
    tokens,
    out_grad,
    block_order,
    qkv_weight,
    proj_weight,
    up_weight,
    down_weight,
    qkv_bias,
    up_bias,
    layer_vectors,
    qkv_first,
    qkv_second,
    proj_first,
    proj_second,
    up_first,
    up_second,
    down_first,
    down_second,
    qbias_first,
    qbias_second,
    ubias_first,
    ubias_second,
    vector_first,
    vector_second,
):
    device = lax.axis_index("ctx")
    groups = lax.axis_size("ctx")
    seqs, rows, width = tokens.shape
    blk = rows // 2
    query_pos = block_positions(block_order, device * rows, rows, blk)
    qkv_full, up_full, proj_full, down_full = (
        lax.all_gather(qkv_weight.astype(jnp.bfloat16), "ctx", axis=0, tiled=True),
        lax.all_gather(up_weight.astype(jnp.bfloat16), "ctx", axis=0, tiled=True),
        lax.all_gather(proj_weight.astype(jnp.bfloat16), "ctx", axis=1, tiled=True),
        lax.all_gather(down_weight.astype(jnp.bfloat16), "ctx", axis=1, tiled=True),
    )
    layer_vector_rows = lax.all_gather(layer_vectors, "ctx", axis=1, tiled=True)
    inputs = tokens.astype(jnp.float32)
    first_normalized, norm_one_back = jax.vjp(
        layer_norm, inputs, layer_vector_rows[0], layer_vector_rows[1]
    )
    normed_low = first_normalized.astype(jnp.bfloat16)
    projection_output = jnp.einsum(
        "sqd,dcf->sqcf", normed_low, qkv_full, preferred_element_type=jnp.float32
    )
    queries = (projection_output[:, :, 0] + qkv_bias[0]).astype(jnp.bfloat16)
    keys = projection_output[:, :, 1].astype(jnp.bfloat16)
    values = (projection_output[:, :, 2] + qkv_bias[1]).astype(jnp.bfloat16)
    heads = queries.shape[-1] // HD
    query_heads = queries.reshape(seqs, rows, heads, HD)
    key_heads = keys.reshape(seqs, rows, heads, HD)
    value_heads = values.reshape(seqs, rows, heads, HD)
    start_state = (
        jnp.full((seqs, heads, rows), -1e30, jnp.float32),
        jnp.zeros((seqs, heads, rows), jnp.float32),
        jnp.zeros((seqs, heads, rows, HD), jnp.float32),
    )
    forward_step = partial(
        forward_fold, queries=query_heads, query_pos=query_pos, order=block_order, blk=blk
    )
    empty_store = jnp.zeros((seqs, rows * groups, keys.shape[-1]), jnp.bfloat16)
    folded, key_store, value_store = keeping_fold(
        (start_state, empty_store, empty_store),
        (
            lax.all_gather(keys, "ctx", axis=1, tiled=True),
            lax.all_gather(values, "ctx", axis=1, tiled=True),
        ),
        jnp.int32(0),
        forward_step=forward_step,
    )
    running_max, running_sum, context_sum = folded
    whole_pair = (key_store, value_store)
    log_total = running_max + jnp.log(running_sum)
    context_value = context_sum / running_sum[..., None]
    context_rows = jnp.transpose(context_value, (0, 2, 1, 3)).reshape(seqs, rows, heads * HD)
    context_low = context_rows.astype(jnp.bfloat16)
    attn_part = jnp.einsum(
        "sqf,fd->sqd", context_low, proj_full, preferred_element_type=jnp.float32
    )
    attention_result = lax.psum(attn_part, "tp") + layer_vector_rows[4]
    middle = inputs + attention_result
    second_normalized, norm_two_back = jax.vjp(
        layer_norm, middle, layer_vector_rows[2], layer_vector_rows[3]
    )
    normed_mid = second_normalized.astype(jnp.bfloat16)
    hidden_preactivation = (
        jnp.einsum("sqd,df->sqf", normed_mid, up_full, preferred_element_type=jnp.float32) + up_bias
    )
    hidden_activation, gelu_back = jax.vjp(gelu_tanh, hidden_preactivation)
    hidden_low = hidden_activation.astype(jnp.bfloat16)
    mlp_part = jnp.einsum("sqf,fd->sqd", hidden_low, down_full, preferred_element_type=jnp.float32)
    mlp_total = lax.psum(mlp_part, "tp") + layer_vector_rows[5]
    block_output = (middle + mlp_total).astype(jnp.bfloat16)
    grad_out = out_grad.astype(jnp.float32)
    grad_down = jnp.einsum("sqf,sqd->fd", hidden_low, out_grad, preferred_element_type=jnp.float32)
    grad_hidden = jnp.einsum("sqd,fd->sqf", out_grad, down_full, preferred_element_type=jnp.float32)
    grad_pre = gelu_back(grad_hidden)[0].astype(jnp.bfloat16)
    grad_up = jnp.einsum("sqd,sqf->df", normed_mid, grad_pre, preferred_element_type=jnp.float32)
    grad_upbias = jnp.sum(grad_pre.astype(jnp.float32), axis=(0, 1))
    mid_part = jnp.einsum("sqf,df->sqd", grad_pre, up_full, preferred_element_type=jnp.float32)
    grad_normed_two = lax.psum(mid_part, "tp")
    grad_mid_norm, grad_gain_two, grad_shift_two = norm_two_back(grad_normed_two)
    grad_middle = grad_out + grad_mid_norm
    grad_attn = grad_middle.astype(jnp.bfloat16)
    grad_proj = jnp.einsum(
        "sqf,sqd->fd", context_low, grad_attn, preferred_element_type=jnp.float32
    )
    grad_context = jnp.einsum(
        "sqd,fd->sqf", grad_attn, proj_full, preferred_element_type=jnp.float32
    ).astype(jnp.bfloat16)
    grad_heads = grad_context.reshape(seqs, rows, heads, HD)
    row_delta = jnp.sum(
        grad_heads.astype(jnp.float32) * context_rows.reshape(seqs, rows, heads, HD), axis=-1
    )
    delta_heads = jnp.transpose(row_delta, (0, 2, 1))
    log_rows = jnp.transpose(log_total, (0, 2, 1))
    zero_heads = jnp.zeros((seqs, heads, rows, HD), jnp.float32)
    query_step = partial(
        query_fold,
        queries=query_heads,
        grad_heads=grad_heads,
        log_total=log_total,
        delta=delta_heads,
        query_pos=query_pos,
        order=block_order,
        blk=blk,
    )
    grad_q_sum = query_step(zero_heads, whole_pair, 0)
    key_step = partial(
        key_fold,
        key_heads=key_heads,
        value_heads=value_heads,
        key_pos=query_pos,
        order=block_order,
        blk=blk,
    )
    grad_k_sum, grad_v_sum = key_step(
        (zero_heads, zero_heads),
        (
            lax.all_gather(queries.astype(jnp.float32), "ctx", axis=1, tiled=True).astype(
                jnp.bfloat16
            ),
            lax.all_gather(grad_context.astype(jnp.float32), "ctx", axis=1, tiled=True).astype(
                jnp.bfloat16
            ),
            lax.all_gather(log_rows, "ctx", axis=1, tiled=True),
            lax.all_gather(row_delta, "ctx", axis=1, tiled=True),
        ),
        jnp.int32(0),
    )

    def head_rows(array):
        return (
            jnp.transpose(array, (0, 2, 1, 3)).reshape(seqs, rows, heads * HD).astype(jnp.bfloat16)
        )

    grad_qkv_low = jnp.stack(
        [head_rows(grad_q_sum), head_rows(grad_k_sum), head_rows(grad_v_sum)], axis=2
    )
    grad_qkv = jnp.einsum(
        "sqd,sqcf->dcf", normed_low, grad_qkv_low, preferred_element_type=jnp.float32
    )
    grad_qbias = jnp.sum(grad_qkv_low[:, :, 0::2].astype(jnp.float32), axis=(0, 1))
    first_part = jnp.einsum(
        "sqcf,dcf->sqd", grad_qkv_low, qkv_full, preferred_element_type=jnp.float32
    )
    grad_normed_one = lax.psum(first_part, "tp")
    grad_in_norm, grad_gain_one, grad_shift_one = norm_one_back(grad_normed_one)
    input_grad = grad_middle + grad_in_norm
    grad_vectors = jnp.stack(
        [
            grad_gain_one,
            grad_shift_one,
            grad_gain_two,
            grad_shift_two,
            jnp.sum(grad_attn.astype(jnp.float32), axis=(0, 1)),
            jnp.sum(grad_out, axis=(0, 1)),
        ]
    )
    sum_qkv, sum_up, sum_proj, sum_down, sum_vectors = (
        lax.psum_scatter(grad_qkv, "ctx", scatter_dimension=0, tiled=True),
        lax.psum_scatter(grad_up, "ctx", scatter_dimension=0, tiled=True),
        lax.psum_scatter(grad_proj, "ctx", scatter_dimension=1, tiled=True),
        lax.psum_scatter(grad_down, "ctx", scatter_dimension=1, tiled=True),
        lax.psum_scatter(grad_vectors, "ctx", scatter_dimension=1, tiled=True),
    )
    sum_qbias, sum_upbias = lax.psum((grad_qbias, grad_upbias), "ctx")
    qkv_new = adamw(qkv_weight, sum_qkv, qkv_first, qkv_second, 0.1, 0.1)
    proj_new = adamw(proj_weight, sum_proj, proj_first, proj_second, 1.0, 0.1)
    up_new = adamw(up_weight, sum_up, up_first, up_second, 0.1, 0.1)
    down_new = adamw(down_weight, sum_down, down_first, down_second, 0.05, 0.1)
    qbias_new = adamw(qkv_bias, sum_qbias, qbias_first, qbias_second, 1.0, 0.0)
    ubias_new = adamw(up_bias, sum_upbias, ubias_first, ubias_second, 1.0, 0.0)
    vector_new = adamw(layer_vectors, sum_vectors, vector_first, vector_second, 1.0, 0.0)
    return (
        block_output,
        input_grad,
        qkv_new[0],
        qkv_new[1],
        qkv_new[2],
        proj_new[0],
        proj_new[1],
        proj_new[2],
        up_new[0],
        up_new[1],
        up_new[2],
        down_new[0],
        down_new[1],
        down_new[2],
        qbias_new[0],
        qbias_new[1],
        qbias_new[2],
        ubias_new[0],
        ubias_new[1],
        ubias_new[2],
        vector_new[0],
        vector_new[1],
        vector_new[2],
    )


def chip_at(place, chips):
    half = chips // 2
    back = place // half
    return (1 - back) * 2 * place + back * (2 * (chips - 1 - place) + 1)


class Ring:
    def __init__(self, chips):
        me = lax.axis_index("ctx")
        self.chips, self.me = chips, me
        self.core = me % 2
        chip = me // 2
        along, across = chip // 2, chip % 2
        self.place = along + across * (chips - 1 - 2 * along)
        self.right, self.left = self.slot(1), self.slot(-1)
        self.mate = chip * 2 + 1 - self.core

    def slot(self, ahead, other=False):
        place = (self.place + ahead + 2 * self.chips) % self.chips
        core = 1 - self.core if other else self.core
        return chip_at(place, self.chips) * 2 + core

    def greet(self, count=3):
        barrier = pltpu.get_barrier_semaphore()
        for device in (self.left, self.right, self.mate):
            pl.semaphore_signal(barrier, inc=1, device_id={"ctx": device}, device_id_type=MESH)
        pl.semaphore_wait(barrier, count)


def remote(src, dst, send, recv, device):
    return pltpu.make_async_remote_copy(
        src_ref=src,
        dst_ref=dst,
        send_sem=send,
        recv_sem=recv,
        device_id={"ctx": device},
        device_id_type=MESH,
    )


class Gather:
    def __init__(self, ring, ins, outs, sems):
        self.ring, self.ins, self.outs = ring, ins, outs
        self.ring_send, self.ring_recv, self.mate_send, self.mate_recv, self.own = sems
        self.far_right = ring.chips // 2
        self.far_left = ring.chips - 1 - self.far_right
        self.sent = []

    def hop(self, at, src, slot, step, sign):
        columns, last = slice(None), step == self.far_right - 1
        if last:
            width = src.shape[-1]
            cut = (width + 128) // 256 * 128
            columns = slice(0, cut) if sign > 0 else slice(cut, width)
        index = step if sign > 0 else self.far_right + step
        return remote(
            src.at[:, columns] if last else src,
            self.outs[at].at[slot, :, columns] if last else self.outs[at].at[slot],
            self.ring_send.at[at, index], self.ring_recv.at[at, index],
            self.ring.right if sign > 0 else self.ring.left,
        )

    def pass_on(self, at, src, slot, index):
        copy = remote(
            src, self.outs[at].at[slot], self.mate_send.at[at, index],
            self.mate_recv.at[at, index], self.ring.mate,
        )
        return copy

    def go(self, copy):
        copy.start()
        self.sent.append(copy)

    def start(self):
        ring = self.ring
        for at, block in enumerate(self.ins):
            self.go(self.hop(at, block, ring.me, 0, 1))
            self.go(self.hop(at, block, ring.me, 0, -1))
            self.go(self.pass_on(at, block, ring.me, 0))
            pltpu.make_async_copy(block, self.outs[at].at[ring.me], self.own.at[at]).start()

    def step(self, step):
        ring = self.ring
        last = step == self.far_right - 1
        for at in range(len(self.ins)):
            for sign in (1, -1):
                slot = ring.slot(-sign * (step + 1))
                block = self.outs[at].at[slot]
                self.hop(at, block, slot, step, sign).wait_recv()
                if not last:
                    self.go(self.hop(at, block, slot, step + 1, sign))
                if not last or sign < 0:
                    index = 1 + step if last or sign > 0 else 1 + self.far_right + step
                    self.go(self.pass_on(at, block, slot, index))

    def finish(self):
        ring = self.ring
        for at in range(len(self.ins)):
            order = [0] + [-(s + 1) for s in range(self.far_right)]
            order += [s + 1 for s in range(self.far_left)]
            for index, ahead in enumerate(order):
                slot = ring.slot(ahead, other=True)
                self.pass_on(at, self.outs[at].at[slot], slot, index).wait_recv()
            pltpu.make_async_copy(
                self.ins[at], self.outs[at].at[ring.me], self.own.at[at]
            ).wait()
        for copy in self.sent:
            copy.wait_send()


def gather_sems(count, chips):
    return [pltpu.SemaphoreType.DMA((count, chips))] * 4 + [pltpu.SemaphoreType.DMA((count,))]


class Scatter:
    def __init__(self, ring, pieces, grads, mates, lands, outs, sems):
        self.ring, self.pieces = ring, pieces
        self.grads, self.mates, self.lands, self.outs = grads, mates, lands, outs
        self.mate_send, self.mate_recv, self.ring_send, self.ring_recv = sems
        self.order = []
        for far in range(1, ring.chips // 2):
            self.order += [-far, far]
        self.order += [ring.chips // 2, 0]
        self.arrived = set()
        self.sent = []

    def to_mate(self, index, at):
        ring = self.ring
        return remote(
            self.grads[at].at[ring.slot(self.order[index], other=True)],
            self.mates[at].at[index],
            self.mate_send.at[at, index], self.mate_recv.at[at, index], ring.mate,
        )

    def start(self):
        for index in range(self.ring.chips):
            for at in range(len(self.grads)):
                copy = self.to_mate(index, at)
                copy.start()
                self.sent.append(copy)

    def own_part(self, ahead, at, columns):
        half = self.ring.chips // 2 - 1
        ahead = (ahead + half) % self.ring.chips - half
        index = self.order.index(ahead)
        if (index, at) not in self.arrived:
            self.arrived.add((index, at))
            self.to_mate(index, at).wait_recv()
        mine = self.grads[at][self.ring.slot(ahead), :, columns].astype(jnp.float32)
        return mine + self.mates[at][index, :, columns].astype(jnp.float32)

    def hop(self, which, step, src):
        device = self.ring.right if self.pieces[which][3] > 0 else self.ring.left
        return remote(
            src, self.lands[which].at[step], self.ring_send.at[which, step],
            self.ring_recv.at[which, step], device,
        )

    def step(self, step):
        chips = self.ring.chips
        for which, (at, first, count, sign) in enumerate(self.pieces):
            columns = slice(first, first + count)
            land = self.lands[which]
            part = self.own_part(-sign * (step + 1), at, columns)
            if step > 0:
                self.hop(which, step - 1, land.at[step - 1]).wait_recv()
                part = part + land[step - 1].astype(jnp.float32)
            if step < chips - 1:
                hold = land.at[chips - 1 + step]
                hold[...] = part.astype(jnp.bfloat16)
                copy = self.hop(which, step, hold)
                copy.start()
                self.sent.append(copy)
            else:
                self.outs[at][:, columns] = part

    def finish(self):
        for copy in self.sent:
            copy.wait_send()


def scatter_scratch(blocks, pieces, chips):
    rows, dma = blocks[0].shape[1], pltpu.SemaphoreType.DMA
    return (
        [pltpu.VMEM((chips, rows, b.shape[2]), jnp.bfloat16) for b in blocks]
        + [pltpu.VMEM((2 * chips - 2, rows, p[2]), jnp.bfloat16) for p in pieces]
        + [dma((len(blocks), chips))] * 2
        + [dma((len(pieces), chips))] * 2
    )


def row_split(array, groups):
    return array.reshape(groups, array.shape[0] // groups, array.shape[1])


def pair_kernel(count, *refs):
    ins, outs = refs[:count], refs[count : 2 * count]
    holds, lands = refs[2 * count : 3 * count], refs[3 * count : 4 * count]
    send, recv = refs[4 * count :]
    other = 1 - lax.axis_index("tp")
    barrier = pltpu.get_barrier_semaphore()
    pl.semaphore_signal(barrier, inc=1, device_id={"tp": other}, device_id_type=MESH)
    for at in range(count):
        holds[at][...] = ins[at][...].astype(jnp.bfloat16)
    pl.semaphore_wait(barrier, 1)
    copies = []
    for at in range(count):
        copy = pltpu.make_async_remote_copy(
            src_ref=holds[at], dst_ref=lands[at], send_sem=send.at[at], recv_sem=recv.at[at],
            device_id={"tp": other}, device_id_type=MESH,
        )
        copy.start()
        copies.append(copy)
    for at in range(count):
        copies[at].wait()
        outs[at][...] = holds[at][...].astype(jnp.float32) + lands[at][...].astype(jnp.float32)


def pair_sum(arrays, collective):
    count = len(arrays)
    vmem = pl.BlockSpec(memory_space=pltpu.VMEM)
    return pl.pallas_call(
        partial(pair_kernel, count),
        out_shape=[jax.ShapeDtypeStruct(a.shape, jnp.float32) for a in arrays],
        in_specs=[vmem] * count,
        out_specs=[vmem] * count,
        scratch_shapes=[pltpu.VMEM(a.shape, jnp.bfloat16) for a in arrays] * 2
        + [pltpu.SemaphoreType.DMA((count,))] * 2,
        compiler_params=pltpu.CompilerParams(
            collective_id=collective, has_side_effects=True, vmem_limit_bytes=VMEM_LIMIT
        ),
    )(*arrays)


NT = (((1,), (1,)), ((), ()))
NN = (((1,), (0,)), ((), ()))


def mul(left, right, dims):
    return lax.dot_general(left, right, dims, preferred_element_type=jnp.float32)


def attend_unit(heads, seq, head, rows, allowed, own, every, context_ref):
    width = heads * HD
    here = slice(seq * rows, (seq + 1) * rows)
    at = slice(head * HD, (head + 1) * HD)
    keys = every[:, here, width + head * HD : width + (head + 1) * HD].reshape(-1, HD)
    values = every[:, here, 2 * width + head * HD : 2 * width + (head + 1) * HD].reshape(-1, HD)
    scores = mul(own(here, at), keys, NT) * 0.125
    scores = jnp.where(allowed, scores, -1000000000.0)
    top = jnp.max(scores, axis=-1, keepdims=True)
    shares = jnp.exp(scores - top)
    total = jnp.sum(shares, axis=-1, keepdims=True)
    mixed = mul(shares.astype(jnp.bfloat16), values, NN)
    context_ref[here, at] = mixed / total
    return top + jnp.log(total)


def front_kernel(chips, heads, *refs):
    ins, (bias, own_pos, all_pos) = refs[0:5], refs[5:8]
    outs, vectors_ref, every, context_ref, log_ref = refs[8:13], *refs[13:17]
    tokens_all, lows, sems = outs[1], refs[17:20], refs[20:]
    width = heads * HD
    groups = 2 * chips
    seqs = own_pos.shape[0]
    rows = tokens_all.shape[1] // seqs
    ring = Ring(chips)
    ring.greet()
    first = Gather(ring, ins[0:2], outs[0:2], sems[0:5])
    second = Gather(ring, lows, outs[2:5], sems[5:10])
    first.start()
    for low, weight in zip(lows, ins[2:5]):
        low[...] = weight[...].astype(jnp.bfloat16)
    for step in range(first.far_right - 1):
        first.step(step)
    second.start()
    first.step(first.far_right - 1)
    first.finish()
    packed = outs[0]
    extra = packed[:, :, 3 * width :].reshape(-1, 128).astype(jnp.float32).T
    vectors = (extra[0:6] + extra[6:12]) + extra[12:18]
    vectors_ref[0:6, :] = vectors
    gain, shift = vectors[0:1], vectors[1:2]

    def project(at, carry):
        values = tokens_all[pl.ds(2 * at, 2)].reshape(-1, tokens_all.shape[2])
        normed = layer_norm(values.astype(jnp.float32), gain, shift).astype(jnp.bfloat16)
        weights = packed[:, :, : 3 * width].reshape(-1, 3 * width)
        result = (mul(normed, weights, NN) + bias[...]).astype(jnp.bfloat16)
        every[pl.ds(2 * at, 2)] = result.reshape(2, -1, 3 * width)
        return carry

    lax.fori_loop(0, groups // 4, project, 0)
    second.step(0)
    lax.fori_loop(groups // 4, groups // 2, project, 0)
    second.step(1)

    def own(here, at):
        return every[ring.me, here, at]

    lanes = lax.broadcasted_iota(jnp.int32, (rows, 128), 1)
    for seq in range(seqs):
        allowed = own_pos[seq] >= all_pos[seq]
        logs = jnp.zeros((rows, 128), jnp.float32)
        for head in range(heads):
            log = attend_unit(heads, seq, head, rows, allowed, own, every, context_ref)
            logs = jnp.where(lanes == head, log, logs)
        log_ref[seq * rows : (seq + 1) * rows, :] = logs
        if seq + 2 < second.far_right:
            second.step(seq + 2)
    for step in range(seqs + 2, second.far_right):
        second.step(step)
    second.finish()


def front(arrays, bias, own_pos, all_pos, heads, groups, collective):
    vmem = pl.BlockSpec(memory_space=pltpu.VMEM)
    hbm = pl.BlockSpec(memory_space=pl.ANY)
    many, width = arrays[1].shape
    chips = groups // 2
    return pl.pallas_call(
        partial(front_kernel, chips, heads),
        out_shape=[jax.ShapeDtypeStruct((groups,) + a.shape, jnp.bfloat16) for a in arrays]
        + [
            jax.ShapeDtypeStruct((8, width), jnp.float32),
            jax.ShapeDtypeStruct((groups, many, 3 * heads * HD), jnp.bfloat16),
            jax.ShapeDtypeStruct((many, heads * HD), jnp.float32),
            jax.ShapeDtypeStruct((many, 128), jnp.float32),
        ],
        in_specs=[vmem] * 8,
        out_specs=[vmem] * 2 + [hbm] * 3 + [vmem] * 4,
        scratch_shapes=[pltpu.VMEM(a.shape, jnp.bfloat16) for a in arrays[2:5]]
        + gather_sems(2, chips)
        + gather_sems(3, chips),
        compiler_params=pltpu.CompilerParams(
            collective_id=collective, has_side_effects=True, vmem_limit_bytes=VMEM_LIMIT
        ),
    )(*arrays, bias, own_pos, all_pos)


def token_sum(array):
    return jnp.sum(array.astype(jnp.float32), axis=0, keepdims=True)


def back_kernel(chips, heads, pieces, lone, *refs):
    own, every, own_pos, all_pos = refs[0:4]
    grad_attn, context, normed_mid, grad_pre, grad_low, hidden = refs[4:10]
    normed, packed, normal, grad_two, normal_two = refs[10:15]
    total, sums, small_out = refs[15], refs[16:20], refs[20]
    out_ref, hold, land, small, gathered = refs[21:26]
    grads, rest = refs[26:30], refs[30:]
    many = len(pieces)
    mates, lands, sems, rest = rest[0:3], rest[3 : 3 + many], rest[3 + many : 7 + many], rest[7 + many :]
    alone = len(lone)
    mate, lone_lands, lone_sems = rest[0:1], rest[1 : 1 + alone], rest[1 + alone : 5 + alone]
    pair_send, pair_recv = rest[5 + alone : 7 + alone]
    gather_one, gather_two = rest[7 + alone : 12 + alone], rest[12 + alone : 17 + alone]
    seqs = own_pos.shape[0]
    rows = own.shape[0] // seqs
    width = heads * HD
    other = 1 - lax.axis_index("tp")
    ring = Ring(chips)
    me = ring.me
    barrier = pltpu.get_barrier_semaphore()
    pl.semaphore_signal(barrier, inc=1, device_id={"tp": other}, device_id_type=MESH)
    ring.greet(4)
    gather = Gather(ring, [own], [gathered], gather_one)
    scatter = Scatter(ring, pieces, grads[0:3], mates, lands, sums[0:3], sems)
    lone_scatter = Scatter(ring, lone, grads[3:4], mate, lone_lands, sums[3:4], lone_sems)

    def product(into, left, right):
        blocks = into.shape[0] // 2
        high = blocks * into.shape[1]
        for half in range(2):
            result = lax.dot_general(
                left[:, half * high : (half + 1) * high], right[...],
                (((0,), (0,)), ((), ())), preferred_element_type=jnp.float32,
            )
            into[half * blocks : (half + 1) * blocks] = result.astype(jnp.bfloat16).reshape(
                (blocks,) + into.shape[1:]
            )

    gather.start()
    product(grads[2], grad_low, hidden)
    gather.step(0)
    product(grads[1], normed_mid, grad_pre)
    gather.step(1)
    product(grads[0], grad_attn, context)
    scatter.start()
    for step in range(2, gather.far_right - 1):
        gather.step(step)
    scatter.step(0)
    gather.step(gather.far_right - 1)
    gather.finish()
    done = 1
    for seq in range(seqs):
        here = slice(seq * rows, (seq + 1) * rows)
        allowed = own_pos[seq] >= all_pos[seq]
        allowed_back = own_pos[seq] <= all_pos[seq]
        stats = gathered[:, here, width:].reshape(-1, 128).astype(jnp.float32).T
        turned = (stats[0:16] + stats[16:32]) + stats[32:48]
        parts = own[here, width:].astype(jnp.float32)
        stat = (parts[:, 0:16] + parts[:, 16:32]) + parts[:, 32:48]
        for head in range(heads):
            at = slice(head * HD, (head + 1) * HD)
            past = slice(width + head * HD, width + (head + 1) * HD)
            last = slice(2 * width + head * HD, 2 * width + (head + 1) * HD)
            queries = every[:, here, at].reshape(-1, HD)
            keys = every[:, here, past].reshape(-1, HD)
            values = every[:, here, last].reshape(-1, HD)
            grad_all = gathered[:, here, at].reshape(-1, HD)
            query, key, value = every[me, here, at], every[me, here, past], every[me, here, last]
            scores = jnp.where(allowed, mul(query, keys, NT) * 0.125, -1000000000.0)
            shares = jnp.exp(scores - stat[:, head : head + 1])
            grad_share = mul(own[here, at], values, NT)
            delta = stat[:, heads + head : heads + head + 1]
            grad_score = (shares * (grad_share - delta)).astype(jnp.bfloat16)
            out_ref[here, at] = (mul(grad_score, keys, NN) * 0.125).astype(jnp.bfloat16)
            scores = jnp.where(allowed_back, mul(key, queries, NT) * 0.125, -1000000000.0)
            shares = jnp.exp(scores - turned[head : head + 1])
            grad_value = mul(shares.astype(jnp.bfloat16), grad_all, NN)
            grad_share = mul(value, grad_all, NT)
            grad_score = shares * (grad_share - turned[heads + head : heads + head + 1])
            grad_key = mul(grad_score.astype(jnp.bfloat16), queries, NN) * 0.125
            out_ref[here, past] = grad_key.astype(jnp.bfloat16)
            out_ref[here, last] = grad_value.astype(jnp.bfloat16)
            if head % 2 == 1 and done < chips - 1:
                scatter.step(done)
                done += 1
    weights = packed[:, :, : 3 * width].reshape(-1, 3 * width)
    hold[...] = mul(out_ref[...], weights, NT).astype(jnp.bfloat16)
    pair = pltpu.make_async_remote_copy(
        src_ref=hold, dst_ref=land, send_sem=pair_send.at[0], recv_sem=pair_recv.at[0],
        device_id={"tp": other}, device_id_type=MESH,
    )
    pair.start()
    product(grads[3], normed, out_ref)
    lone_scatter.start()
    if done < chips:
        scatter.step(done)
    lone_scatter.step(0)
    small[...] = jnp.zeros_like(small)
    small[2:3, :] = jnp.sum(grad_two[...] * normal_two[...], axis=0, keepdims=True)
    small[3:4, :] = token_sum(grad_two[...])
    small[4:5, :] = token_sum(grad_attn[...])
    small[5:6, :] = token_sum(grad_low[...])
    small[6:7, 0:width] = token_sum(out_ref[:, 0:width])
    small[7:8, 0:width] = token_sum(out_ref[:, 2 * width : 3 * width])
    span = small.shape[1]
    for at in range(grad_pre.shape[1] // span):
        small[8 + at : 9 + at, :] = token_sum(grad_pre[:, at * span : (at + 1) * span])
    pair.wait()
    summed = hold[...].astype(jnp.float32) + land[...].astype(jnp.float32)
    total[...] = summed
    small[0:1, :] = jnp.sum(summed * normal[...], axis=0, keepdims=True)
    small[1:2, :] = token_sum(summed)
    last = Gather(ring, [small], [small_out], gather_two)
    last.start()
    for step in range(1, chips):
        if done + step < chips:
            scatter.step(done + step)
        lone_scatter.step(step)
        if step - 1 < last.far_right:
            last.step(step - 1)
    for step in range(chips - 1, last.far_right):
        last.step(step)
    last.finish()
    scatter.finish()
    lone_scatter.finish()


def back(arrays, widths, heads, groups, collective):
    vmem = pl.BlockSpec(memory_space=pltpu.VMEM)
    dma = pltpu.SemaphoreType.DMA
    chips = groups // 2
    own = arrays[0]
    many, width = arrays[4].shape
    blocks = [jax.ShapeDtypeStruct((groups, width // groups, w), jnp.bfloat16) for w in widths]
    proj, up, down, qkv = widths
    cut = proj * 2 // 3 // 128 * 128
    pieces = ((1, 0, up, 1), (2, 0, down, -1), (0, 0, cut, 1), (0, cut, proj - cut, -1))
    right = qkv // 256 * 128
    lone = ((0, 0, right, 1), (0, right, qkv - right, -1))
    small = (8 + -(-up // width) + 7) // 8 * 8, width
    return pl.pallas_call(
        partial(back_kernel, chips, heads, pieces, lone),
        out_shape=[jax.ShapeDtypeStruct((many, width), jnp.float32)]
        + [jax.ShapeDtypeStruct(b.shape[1:], jnp.float32) for b in blocks]
        + [jax.ShapeDtypeStruct((groups,) + small, jnp.float32)],
        in_specs=[vmem] * 15,
        out_specs=[vmem] * 6,
        scratch_shapes=[
            pltpu.VMEM((many, qkv), jnp.bfloat16),
            pltpu.VMEM((many, width), jnp.bfloat16),
            pltpu.VMEM((many, width), jnp.bfloat16),
            pltpu.VMEM(small, jnp.float32),
            pltpu.VMEM((groups,) + own.shape, own.dtype),
        ]
        + [pltpu.VMEM(b.shape, b.dtype) for b in blocks]
        + scatter_scratch(blocks[0:3], pieces, chips)
        + scatter_scratch(blocks[3:4], lone, chips)
        + [dma((1,)), dma((1,))]
        + gather_sems(1, chips)
        + gather_sems(1, chips),
        compiler_params=pltpu.CompilerParams(
            collective_id=collective, has_side_effects=True, vmem_limit_bytes=VMEM_LIMIT
        ),
    )(*arrays)


def standard(values):
    center = values - jnp.mean(values, axis=-1, keepdims=True)
    spread = jnp.mean(center * center, axis=-1, keepdims=True)
    return center * lax.rsqrt(spread + 1e-05)


def three_parts(array):
    high = lax.reduce_precision(array, 8, 7)
    rest = array - high
    middle = lax.reduce_precision(rest, 8, 7)
    return [part.astype(jnp.bfloat16) for part in (high, middle, rest - middle)]


def ring_local(
    tokens,
    out_grad,
    block_order,
    qkv_weight,
    proj_weight,
    up_weight,
    down_weight,
    qkv_bias,
    up_bias,
    layer_vectors,
    qkv_first,
    qkv_second,
    proj_first,
    proj_second,
    up_first,
    up_second,
    down_first,
    down_second,
    qbias_first,
    qbias_second,
    ubias_first,
    ubias_second,
    vector_first,
    vector_second,
):
    device = lax.axis_index("ctx")
    groups = lax.axis_size("ctx")
    seqs, rows, width = tokens.shape
    blk = rows // 2
    share = qkv_weight.shape[0]
    inner = qkv_weight.shape[2]
    heads = inner // HD
    many = seqs * rows
    own_pos = block_positions(block_order, device * rows, rows, blk)[:, :, None]
    all_pos = block_positions(block_order, 0, rows * groups, blk)[:, None, :]
    low = jnp.bfloat16
    vector_parts = jnp.concatenate(three_parts(layer_vectors.T), axis=1)
    packed = jnp.concatenate(
        [
            qkv_weight.astype(low).reshape(share, 3 * inner),
            jnp.pad(vector_parts, ((0, 0), (0, 128 - vector_parts.shape[1]))),
        ],
        axis=1,
    )
    bias = jnp.concatenate([qkv_bias[0], jnp.zeros_like(qkv_bias[0]), qkv_bias[1]])[None]
    grad_low = out_grad.reshape(many, width)
    packed_full, _, proj_full, up_full, down_full, vectors, every, context, logs = front(
        [
            packed,
            tokens.reshape(many, width),
            proj_weight.T,
            up_weight,
            down_weight.T,
        ],
        bias,
        own_pos,
        all_pos,
        heads,
        groups,
        1,
    )
    proj_full = proj_full.reshape(width, -1)
    up_full = up_full.reshape(width, -1)
    down_full = down_full.reshape(width, -1)
    inputs = tokens.reshape(many, width).astype(jnp.float32)
    first_normalized, norm_one_back = jax.vjp(layer_norm, inputs, vectors[0], vectors[1])
    normed_low = first_normalized.astype(low)
    normal = standard(inputs)
    context_low = context.astype(low)
    (attn,) = pair_sum([mul(context_low, proj_full, NT)], 3)
    middle = inputs + (attn + vectors[4])
    second_normalized, norm_two_back = jax.vjp(layer_norm, middle, vectors[2], vectors[3])
    normed_mid = second_normalized.astype(low)
    normal_two = standard(middle)
    hidden_preactivation = mul(normed_mid, up_full, NN) + up_bias
    hidden_activation, gelu_back = jax.vjp(gelu_tanh, hidden_preactivation)
    hidden_low = hidden_activation.astype(low)
    grad_hidden = mul(grad_low, down_full, NN)
    grad_pre = gelu_back(grad_hidden)[0].astype(low)
    mlp, grad_normed_two = pair_sum(
        [mul(hidden_low, down_full, NT), mul(grad_pre, up_full, NT)], 4
    )
    block_output = (middle + (mlp + vectors[5])).astype(low)
    grad_out = grad_low.astype(jnp.float32)
    grad_mid_norm = norm_two_back(grad_normed_two)[0]
    grad_middle = grad_out + grad_mid_norm
    grad_attn = grad_middle.astype(low)
    grad_context = mul(grad_attn, proj_full, NN).astype(low)
    lanes = jnp.arange(128)[None, :]
    choose = (lanes == heads + jnp.arange(inner)[:, None] // HD).astype(jnp.float32)
    delta = jnp.dot(
        grad_context.astype(jnp.float32) * context, choose, precision=lax.Precision.HIGHEST
    )
    stats = three_parts((logs + delta)[:, :16])
    own = jnp.concatenate([grad_context] + stats + [jnp.zeros((many, 80), low)], axis=1)

    grad_normed_one, sum_proj, sum_up, sum_down, sum_qkv, all_small = back(
        [
            own, every, own_pos, all_pos,
            grad_attn, context_low, normed_mid, grad_pre, grad_low, hidden_low,
            normed_low, packed_full, normal, grad_normed_two, normal_two,
        ],
        (inner, up_full.shape[1], down_full.shape[1], 3 * inner),
        heads,
        groups,
        5,
    )
    grad_in_norm = norm_one_back(grad_normed_one)[0]
    input_grad = grad_middle + grad_in_norm
    sums = jnp.sum(all_small, axis=0)
    sum_vectors = lax.dynamic_slice_in_dim(sums[0:6], device * share, share, 1)
    sum_qbias = sums[6:8, :inner]
    sum_upbias = sums[8:].reshape(-1)[: up_bias.shape[0]]
    qkv_new = adamw(
        qkv_weight, sum_qkv.reshape(share, 3, inner), qkv_first, qkv_second, 0.1, 0.1
    )
    proj_new = adamw(proj_weight, sum_proj.T, proj_first, proj_second, 1.0, 0.1)
    up_new = adamw(up_weight, sum_up, up_first, up_second, 0.1, 0.1)
    down_new = adamw(down_weight, sum_down.T, down_first, down_second, 0.05, 0.1)
    qbias_new = adamw(qkv_bias, sum_qbias, qbias_first, qbias_second, 1.0, 0.0)
    ubias_new = adamw(up_bias, sum_upbias, ubias_first, ubias_second, 1.0, 0.0)
    vector_new = adamw(layer_vectors, sum_vectors, vector_first, vector_second, 1.0, 0.0)
    return (
        block_output.reshape(seqs, rows, width),
        input_grad.reshape(seqs, rows, width),
        *qkv_new,
        *proj_new,
        *up_new,
        *down_new,
        *qbias_new,
        *ubias_new,
        *vector_new,
    )


def solution(mesh):
    groups = mesh.shape["ctx"]
    tiled = groups >= 16 and groups % 4 == 0 and WIDTH % (groups * 16) == 0
    return jax.shard_map(
        ring_local if tiled else local,
        mesh=mesh,
        in_specs=(
            P(None, "ctx", None),
            P(None, "ctx", None),
            P(),
            P("ctx", None, "tp"),
            P("tp", "ctx"),
            P("ctx", "tp"),
            P("tp", "ctx"),
            P(None, "tp"),
            P("tp"),
            P(None, "ctx"),
            P("ctx", None, "tp"),
            P("ctx", None, "tp"),
            P("tp", "ctx"),
            P("tp", "ctx"),
            P("ctx", "tp"),
            P("ctx", "tp"),
            P("tp", "ctx"),
            P("tp", "ctx"),
            P(None, "tp"),
            P(None, "tp"),
            P("tp"),
            P("tp"),
            P(None, "ctx"),
            P(None, "ctx"),
        ),
        out_specs=(
            P(None, "ctx", None),
            P(None, "ctx", None),
            P("ctx", None, "tp"),
            P("ctx", None, "tp"),
            P("ctx", None, "tp"),
            P("tp", "ctx"),
            P("tp", "ctx"),
            P("tp", "ctx"),
            P("ctx", "tp"),
            P("ctx", "tp"),
            P("ctx", "tp"),
            P("tp", "ctx"),
            P("tp", "ctx"),
            P("tp", "ctx"),
            P(None, "tp"),
            P(None, "tp"),
            P(None, "tp"),
            P("tp"),
            P("tp"),
            P("tp"),
            P(None, "ctx"),
            P(None, "ctx"),
            P(None, "ctx"),
        ),
        check_vma=False,
    )
```
